256 devices in a mesh: ctx: 32 (over y, z), tp: 8 (over x, core).
Axes of the slice: x: 4, y: 4, z: 8, core: 2. Of those that a mesh axis runs over, the one named last changes fastest.
Arguments:
- tokens: bfloat16 [49152, 2048], P('ctx', 'tp')
- router: bfloat16 [2048], P('tp'), may hold values from -0.125 to 0.125
- gain: bfloat16 [2048], P('tp'), may hold values from 0.5 to 1.5
- w_query: bfloat16 [2048, 2048], P(None, 'tp')
- w_key: bfloat16 [2048, 2048], P(None, 'tp')
- w_value: bfloat16 [2048, 2048], P(None, 'tp'), may hold values from -0.125 to 0.125
- w_out: bfloat16 [2048, 2048], P('tp'), may hold values from -0.375 to 0.375
- counts: int32 [32], replicated, may hold values from 0 to 384, as said below
- picked: int32 [32, 384], replicated, may hold values from 0 to 49151, as said below
Outputs:
- update: bfloat16 [12288, 2048], P('ctx', 'tp')
The draws below stay inside these ranges and needn't reach their ends.
Inputs may be any that keep to these rules, and one draw needn't show every extreme that they name: The counts sum to 6144; some index holds exactly 384. `picked`: row c holds distinct positions from c * 1536 to (c + 1) * 1536 - 1, in no particular order; only the first counts[c] entries are selected.
All inputs are finite; a program needn't handle non-finite values.
Results may differ from the reference program's by a relative error of at most 0.02.
Values may be sent and summed in bfloat16 or wider, within the bound.
A program may use at most 256 MiB of HBM per device.

```python
import math
import jax
import jax.numpy as jnp
from jax import lax

D = 2048
H = 32
HD = 64
SEQ_DEV = 1536
MEAN = 192
CAP = 384
TOKENS = 49152
SLOTS = 12288
SELECTED = 6144
N_CTX = 32


def query_base(key):
    return jax.random.normal(key, (D, D), jnp.float32) * math.sqrt(2.0 / D)


def draw_w_query(key, part):
    shared = query_base(key)
    return shared.astype(jnp.bfloat16)


def draw_w_key(key, part):
    key = jax.random.fold_in(key, 4)
    fresh = jax.random.normal(key, (D, D), jnp.float32) * math.sqrt(2.0 / D)
    return fresh.astype(jnp.bfloat16)


def draw_tokens(key, part):
    key = jax.random.fold_in(key, 5)
    return jax.random.normal(key, (TOKENS, D), jnp.float32).astype(jnp.bfloat16)


def draw_counts(key, part):
    key = jax.random.fold_in(key, 6)
    order = jax.random.permutation(jax.random.fold_in(key, 1), N_CTX)
    spread = jax.random.randint(jax.random.fold_in(key, 2), (N_CTX // 2,), 0, MEAN + 1)
    spread = spread.at[0].set(MEAN)
    paired = jnp.concatenate([MEAN + spread, MEAN - spread]).astype(jnp.int32)
    return jnp.zeros((N_CTX,), jnp.int32).at[order].set(paired)


def draw_picked(key, part):
    key = jax.random.fold_in(key, 7)
    sub_keys = jax.random.split(key, N_CTX)
    shuffled = jax.vmap(lambda single: jax.random.permutation(single, SEQ_DEV))(sub_keys)[:, :CAP]
    offsets = jnp.arange(N_CTX, dtype=jnp.int32)[:, None] * SEQ_DEV
    return (shuffled.astype(jnp.int32) + offsets).astype(jnp.int32)


def block_levels(own_key, dims, pieces, least, high):
    level, own = 1.0, jax.random.fold_in(own_key, 6)
    for position, shards_of in pieces:
        draws = jnp.exp(jax.random.uniform(jax.random.fold_in(own, position), (shards_of,), jnp.float32, least / len(pieces), high / len(pieces)))
        level = level * jnp.repeat(draws, dims[position] // shards_of).reshape([-1 if axis == position else 1 for axis in range(len(dims))])
    return level


def normal_values(stream_key, shape, deviation, most, cuts=(), kind=jnp.bfloat16):
    entries = jax.random.normal(stream_key, shape, jnp.float32) * deviation
    if len(cuts) > 0:
        entries = block_levels(stream_key, shape, cuts, -0.22, 0.18) * entries
    return jnp.clip(entries, min=-most, max=most).astype(kind)


def setup_inputs(seed: int = 0) -> dict:
    key_of = jax.random.split(jax.random.key(seed), 10)
    return {
        "tokens": draw_tokens(jax.random.fold_in(key_of[9], 71), 0),
        "router": normal_values(key_of[1], (D,), D ** -0.5, 0.125, ((0, 8),)),
        "gain": jnp.clip(1.0 + 0.1 * jax.random.normal(key_of[2], (D,), jnp.float32), 0.5, 1.5).astype(jnp.bfloat16),
        "w_query": draw_w_query(jax.random.fold_in(key_of[9], 71), 0),
        "w_key": draw_w_key(jax.random.fold_in(key_of[9], 71), 0),
        "w_value": normal_values(key_of[5], (D, D), D ** -0.5, 0.125, ((1, 8),)),
        "w_out": normal_values(key_of[6], (D, D), (D // 8) ** -0.5, 0.375, ((0, 8),)),
        "counts": draw_counts(jax.random.fold_in(key_of[9], 71), 0),
        "picked": draw_picked(jax.random.fold_in(key_of[9], 71), 0),
    }


NEG_FILL = -1e+30
EPSILON = 1e-05

def one_head(queries, keys, values, places):
    scores = jnp.dot(queries, keys.T, preferred_element_type=jnp.float32) * (1.0 / math.sqrt(HD))
    allowed = places[None, :] <= places[:, None]
    scores = jnp.where(allowed, scores, NEG_FILL)
    peak = lax.optimization_barrier(jnp.max(scores, axis=1, keepdims=True))
    weights = jnp.where(allowed, jnp.exp(scores - peak), 0.0)
    denom = lax.optimization_barrier(jnp.sum(weights, axis=1))
    summed = jnp.dot(weights.astype(jnp.bfloat16), values, preferred_element_type=jnp.float32)
    return (summed / denom[:, None]).astype(jnp.bfloat16)

def reference(tokens, router, gain, w_query, w_key, w_value, w_out, counts, picked):
    slot_ids = jnp.arange(CAP, dtype=jnp.int32)
    live_flat = (slot_ids[None, :] < counts[:, None]).reshape(-1)
    chosen = jnp.nonzero(live_flat, size=SELECTED)[0].astype(jnp.int32)
    places = picked.reshape(-1)[chosen]
    sel_rows = tokens[places]
    widened = sel_rows.astype(jnp.float32)
    route = jnp.dot(sel_rows, router, preferred_element_type=jnp.float32)
    gating = jax.nn.sigmoid(route)
    norm_scale = lax.rsqrt(lax.optimization_barrier(jnp.mean(widened * widened, axis=1)) + EPSILON)
    normed = (widened * norm_scale[:, None] * gain.astype(jnp.float32)).astype(jnp.bfloat16)
    queries = jnp.dot(normed, w_query, preferred_element_type=jnp.float32).astype(jnp.bfloat16)
    keys = jnp.dot(normed, w_key, preferred_element_type=jnp.float32).astype(jnp.bfloat16)
    values = jnp.dot(normed, w_value, preferred_element_type=jnp.float32).astype(jnp.bfloat16)

    def split_heads(matrix):
        return matrix.reshape(SELECTED, H, HD).transpose(1, 0, 2)

    def per_head(group):
        return one_head(group[0], group[1], group[2], places)
    attended = lax.map(per_head, (split_heads(queries), split_heads(keys), split_heads(values)))
    attended = attended.transpose(1, 0, 2).reshape(SELECTED, D)
    projected = jnp.dot(attended, w_out, preferred_element_type=jnp.float32)
    gated = (gating[:, None] * projected).astype(jnp.bfloat16)
    return jnp.zeros((SLOTS, D), jnp.bfloat16).at[chosen].set(gated)
```

```python
import functools
import math

import jax
import jax.numpy as jnp
from jax import lax
from jax.experimental import pallas as pl
from jax.experimental.pallas import tpu as pltpu
from jax.sharding import PartitionSpec as P

HD = 64
EPSILON = 1e-05
NEG_FILL = -1e30
MESH = pl.DeviceIdType.MESH
BF16 = jnp.bfloat16
F32 = jnp.float32
I32 = jnp.int32


def iota(shape, dim):
    return lax.broadcasted_iota(I32, shape, dim)


def one_hot(mask):
    return jnp.where(mask, 1.0, 0.0).astype(BF16)


def dot(a, b):
    return jnp.dot(a, b, preferred_element_type=F32)


def dot_t(a, b):
    return lax.dot_general(a, b, (((1,), (1,)), ((), ())), preferred_element_type=F32)


def remote(src, dst, send, recv, **where):
    return pltpu.make_async_remote_copy(
        src_ref=src, dst_ref=dst, send_sem=send, recv_sem=recv, device_id=where, device_id_type=MESH
    )


def kernel(
    cfg,
    counts_ref,
    picked_ref,
    tokens_ref,
    extra_ref,
    wq_hbm,
    wk_hbm,
    wv_hbm,
    wo_hbm,
    out_ref,
    wq_ref,
    wk_ref,
    wv_ref,
    wo_ref,
    row_send,
    row_recv,
    gathered,
    normed_ref,
    kv_send,
    kv_ref,
    q_send,
    q_recv,
    q_ref,
    max_ref,
    sum_ref,
    acc_ref,
    att_send,
    att_recv,
    pair_send,
    pair_recv,
    own_ref,
    part_send,
    part_recv,
    back_send,
    back_recv,
    w_sem,
    row_ss,
    row_rs,
    gat_ss,
    gat_rs,
    kvy_ss,
    kvy_rs,
    qy_ss,
    qy_rs,
    right_ss,
    right_rs,
    left_ss,
    left_rs,
    att_ss,
    att_rs,
    pair_ss,
    pair_rs,
    part_ss,
    part_rs,
    back_ss,
    back_rs,
):
    ny, nz, nx = cfg["ny"], cfg["nz"], cfg["nx"]
    rows, chunk, blocks = cfg["rows"], cfg["chunk"], cfg["blocks"]
    ctx, tp = ny * nz, nx * 2
    seq, feats = tokens_ref.shape
    cap = picked_ref.shape[1]
    slots = ctx * chunk
    half = rows // 2
    width = feats * tp

    c = lax.axis_index("ctx")
    t = lax.axis_index("tp")
    y, z = c // nz, lax.rem(c, nz)
    x, core = t // 2, lax.rem(t, 2)
    sibling = x * 2 + 1 - core

    barrier = pltpu.get_barrier_semaphore()

    def greet(i, _):
        pl.semaphore_signal(
            barrier, inc=1, device_id={"ctx": lax.rem(c + i, ctx)}, device_id_type=MESH
        )
        return 0

    lax.fori_loop(1, ctx, greet, 0)
    for dx in range(1, nx):
        pl.semaphore_signal(
            barrier,
            inc=1,
            device_id={"tp": lax.rem(x + dx, nx) * 2 + core},
            device_id_type=MESH,
        )
    pl.semaphore_signal(barrier, inc=1, device_id={"tp": sibling}, device_id_type=MESH)

    weight_copies = [
        pltpu.make_async_copy(src, dst, w_sem.at[i])
        for i, (src, dst) in enumerate(
            ((wq_hbm, wq_ref), (wk_hbm, wk_ref), (wv_hbm, wv_ref), (wo_hbm, wo_ref))
        )
    ]
    for copy in weight_copies:
        copy.start()

    own_count = counts_ref[c]
    own_offset = jnp.int32(0)
    for i in range(ctx):
        own_offset = own_offset + jnp.where(i < c, counts_ref[i], 0)
    place_row = picked_ref[pl.ds(c, 1), :] - c * seq
    place_full = jnp.broadcast_to(place_row, (cap, cap)).T
    live_row = iota((1, cap), 1) < own_count
    live_col = iota((cap, 1), 0) < own_count
    before_col = jnp.where(live_row & (place_row < place_full), 1.0, 0.0)
    before_row = jnp.where(live_col & (place_full < place_row), 1.0, 0.0)
    order_col = jnp.where(live_col, jnp.sum(before_col, axis=1, keepdims=True).astype(I32), -1)
    order_row = jnp.where(live_row, jnp.sum(before_row, axis=0, keepdims=True).astype(I32), -1)

    def wanted(index):
        dest, number = index // chunk, lax.rem(index, chunk)
        return ((dest - own_offset) & (ctx - 1)) + ctx * number

    deal = one_hot(wanted(iota((slots, cap), 0)) == order_row)
    undeal = one_hot(wanted(iota((cap, slots), 1)) == order_col)
    pick = one_hot(place_full[:, :1] == iota((cap, seq), 1))
    picked_rows = dot(pick, tokens_ref[...]).astype(BF16)
    row_send[...] = dot(deal, picked_rows).astype(BF16)

    pl.semaphore_wait(barrier, ctx - 1 + nx)

    def span(i):
        return pl.ds(pl.multiple_of(i * chunk, chunk), chunk)

    def exchange(send_ref, recv_ref, ss, rs):
        def begin(i, _):
            d = lax.rem(c + i, ctx)
            remote(
                send_ref.at[span(d)], recv_ref.at[span(c)], ss.at[d], rs.at[c], ctx=d
            ).start()
            return 0

        lax.fori_loop(1, ctx, begin, 0)
        recv_ref[span(c), :] = send_ref[span(c), :]

    def exchange_wait(send_ref, recv_ref, ss, rs):
        def end(i, _):
            d = lax.rem(c + i, ctx)
            remote(send_ref.at[span(d)], recv_ref.at[span(d)], ss.at[d], rs.at[d], ctx=d).wait()
            return 0

        lax.fori_loop(1, ctx, end, 0)

    exchange(row_send, row_recv, row_ss, row_rs)

    source = iota((8, slots), 1) // chunk
    offset_of = jnp.zeros((8, slots), I32)
    count_of = jnp.zeros((8, slots), I32)
    for i in range(ctx):
        count = counts_ref[i]
        offset_of = offset_of + jnp.where(source > i, count, 0)
        count_of = count_of + jnp.where(source == i, count, 0)
    number = ((c - offset_of) & (ctx - 1)) + ctx * lax.rem(iota((8, slots), 1), chunk)
    local_index = jnp.where(number < count_of, (offset_of + number - c) // ctx, -1)
    compact = one_hot(local_index[:1] == iota((rows, slots), 0))
    spread_index = jnp.broadcast_to(local_index[:1], (128, slots)).T[:, :1]
    spread = one_hot(spread_index == iota((slots, rows), 1))

    exchange_wait(row_send, row_recv, row_ss, row_rs)

    gathered[t, pl.ds(0, rows), :] = dot(compact, row_recv[...]).astype(BF16)
    gathered[t, pl.ds(rows, 16), :] = extra_ref[...]

    def gather_copy(block, slot, target):
        return remote(
            gathered.at[block], gathered.at[block], gat_ss.at[slot], gat_rs.at[block], tp=target
        )

    sends = []
    for dx in sorted(range(1, nx), key=lambda d: -min(d, nx - d)):
        sends.append(gather_copy(t, dx - 1, lax.rem(x + dx, nx) * 2 + core))
    sends.append(gather_copy(t, nx - 1, sibling))
    for copy in sends:
        copy.start()
    for dx in sorted(range(1, nx), key=lambda d: min(d, nx - d)):
        block = lax.rem(x + nx - dx, nx) * 2 + core
        gather_copy(block, nx - 1 + dx, sibling).wait_recv()
        onward = gather_copy(block, nx - 1 + dx, sibling)
        onward.start()
        sends.append(onward)
    for other in range(nx):
        gather_copy(other * 2 + 1 - core, 0, sibling).wait_recv()
    for copy in sends:
        copy.wait_send()

    squares = jnp.zeros((rows, feats), F32)
    routes = jnp.zeros((rows, feats), F32)
    for b in range(tp):
        wide = gathered[b, pl.ds(0, rows), :].astype(F32)
        params = gathered[b, pl.ds(rows, 16), :].astype(F32)
        squares = squares + wide * wide
        routes = routes + wide * params[1:2]
    scale = lax.rsqrt(jnp.sum(squares, axis=1, keepdims=True) / width + EPSILON)
    gating = 1.0 / (1.0 + jnp.exp(-jnp.sum(routes, axis=1, keepdims=True)))
    for b in range(tp):
        wide = gathered[b, pl.ds(0, rows), :].astype(F32)
        params = gathered[b, pl.ds(rows, 16), :].astype(F32)
        normed_ref[:, pl.ds(b * feats, feats)] = (wide * scale * params[0:1]).astype(BF16)

    for copy in weight_copies:
        copy.wait()
    normed = normed_ref[...]
    keys = dot(normed, wk_ref[...]).astype(BF16)
    values = dot(normed, wv_ref[...]).astype(BF16)
    for h in range(ny):
        cols = slice(h * HD, (h + 1) * HD)
        kv_send[h] = jnp.concatenate([keys[:, cols], values[:, cols]], axis=1)

    def across_y(send_ref, target, recv_slot, ss, rs, dy):
        other = lax.rem(y + dy, ny)
        return remote(send_ref.at[other], target(recv_slot), ss.at[dy], rs.at[recv_slot], ctx=other * nz + z)

    steps = sorted(range(1, ny), key=lambda d: -min(d, ny - d))
    kv_slot = lambda s: kv_ref.at[z, s]
    q_slot = lambda s: q_recv.at[s]
    att_slot = lambda s: att_recv.at[s]
    for dy in steps:
        across_y(kv_send, kv_slot, y, kvy_ss, kvy_rs, dy).start()
    kv_ref[z, y] = kv_send[y]

    queries = (dot(normed, wq_ref[...]).astype(BF16).astype(F32) * (1.0 / math.sqrt(HD))).astype(BF16)
    for h in range(ny):
        cols = slice(h * HD, (h + 1) * HD)
        q_send[h] = jnp.concatenate([queries[:half, cols], queries[half:, cols]], axis=1)
    for dy in steps:
        across_y(q_send, q_slot, y, qy_ss, qy_rs, dy).start()
    q_recv[y] = q_send[y]

    right = y * nz + lax.rem(z + 1, nz)
    left = y * nz + lax.rem(z + nz - 1, nz)
    far = nz // 2

    def ring_copy(to_right, step, slab):
        if to_right:
            origin = lax.rem(z + nz - step, nz)
            ss, rs, target = right_ss, right_rs, right
        else:
            origin = lax.rem(z + step, nz)
            ss, rs, target = left_ss, left_rs, left
        view = kv_ref.at[origin, slab]
        return remote(view, view, ss.at[step, slab], rs.at[step, slab], ctx=target)

    def hops(to_right, slab):
        return far if (slab < ny // 2) == to_right else far - 1

    ring_sends = []

    def forward(step, slab, to_right):
        if step < hops(to_right, slab):
            copy = ring_copy(to_right, step, slab)
            copy.start()
            ring_sends.append(copy)

    def arrived(step, slab, to_right):
        if step <= hops(to_right, slab):
            view = kv_ref.at[lax.rem(z + (nz - step if to_right else step), nz), slab]
            ss, rs = (right_ss, right_rs) if to_right else (left_ss, left_rs)
            remote(
                view, view, ss.at[step - 1, slab], rs.at[step - 1, slab], ctx=right if to_right else left
            ).wait_recv()

    for dy in range(1, ny):
        other = lax.rem(y + dy, ny)
        remote(
            kv_send.at[other], kv_ref.at[z, other], kvy_ss.at[dy], kvy_rs.at[other], ctx=other * nz + z
        ).wait()
    for slab in range(ny):
        for to_right in (True, False):
            forward(0, slab, to_right)
    for dy in range(1, ny):
        other = lax.rem(y + dy, ny)
        remote(
            q_send.at[other], q_recv.at[other], qy_ss.at[dy], qy_rs.at[other], ctx=other * nz + z
        ).wait()

    zeros = jnp.zeros((half, HD), BF16)
    for s in range(ny):
        packed = q_recv[s]
        q_ref[s, pl.ds(0, half), :] = jnp.concatenate([packed[:, :HD], zeros], axis=1)
        q_ref[s, pl.ds(half, half), :] = jnp.concatenate([packed[:, HD:], zeros], axis=1)

    size = rows // blocks
    tile = ny * size
    tile_row = iota((tile, 1), 0)
    tile_col = iota((1, tile), 1)
    query_key = lax.rem(tile_row, size) * ctx + (tile_row // size) * nz + z
    key_base = lax.rem(tile_col, size) * ctx + (tile_col // size) * nz

    def attend(origin, first):
        allowed = key_base + origin <= query_key
        for b in range(blocks):
            q = q_ref[:, pl.ds(b * size, size), :].reshape(tile, 2 * HD)
            near = kv_ref[origin, :, pl.ds(b * size, size), :].reshape(tile, 2 * HD)
            near_score = jnp.where(allowed, dot_t(q, near), NEG_FILL)
            peak = jnp.max(near_score, axis=1, keepdims=True)
            if b:
                past = kv_ref[origin, :, pl.ds(0, b * size), :].reshape(b * tile, 2 * HD)
                past_score = dot_t(q, past)
                peak = jnp.maximum(peak, jnp.max(past_score, axis=1, keepdims=True))
            if not first:
                old = max_ref[b]
                peak = jnp.maximum(old, peak)
                shrink = jnp.exp(old - peak)
            near_weight = jnp.where(allowed, jnp.exp(near_score - peak), 0.0)
            total = jnp.sum(near_weight, axis=1, keepdims=True)
            product = dot(near_weight.astype(BF16), near)
            if b:
                past_weight = jnp.exp(past_score - peak)
                total = total + jnp.sum(past_weight, axis=1, keepdims=True)
                product = product + dot(past_weight.astype(BF16), past)
            if not first:
                total = total + sum_ref[b] * shrink
                product = product + acc_ref[b] * shrink
            max_ref[b] = peak
            sum_ref[b] = total
            acc_ref[b] = product

    attend(z, True)
    for step in range(1, far + 1):
        for slab in range(ny):
            for to_right in (True, False):
                arrived(step, slab, to_right)
                forward(step, slab, to_right)
        if step < far:

            def both(i, _):
                attend(lax.rem(z + jnp.where(i == 0, nz - step, step), nz), False)
                return 0

            lax.fori_loop(0, 2, both, 0)
        else:
            attend(lax.rem(z + far, nz), False)
    for copy in ring_sends:
        copy.wait_send()

    for b in range(blocks):
        result = (acc_ref[b] / sum_ref[b]).astype(BF16).reshape(ny, size, 2 * HD)
        q_ref[:, pl.ds(b * size, size), :] = result
    for s in range(ny):
        att_send[s] = jnp.concatenate(
            [q_ref[s, pl.ds(0, half), :][:, HD:], q_ref[s, pl.ds(half, half), :][:, HD:]], axis=1
        )
    for dy in steps:
        across_y(att_send, att_slot, y, att_ss, att_rs, dy).start()
    att_recv[y] = att_send[y]
    for dy in range(1, ny):
        other = lax.rem(y + dy, ny)
        remote(
            att_send.at[other], att_recv.at[other], att_ss.at[dy], att_rs.at[other], ctx=other * nz + z
        ).wait()
    joined = [att_recv[h] for h in range(ny)]
    attended = jnp.concatenate(
        [
            jnp.concatenate([packed[:, :HD] for packed in joined], axis=1),
            jnp.concatenate([packed[:, HD:] for packed in joined], axis=1),
        ],
        axis=0,
    )

    def columns(index):
        return pl.ds(pl.multiple_of(index * feats, feats), feats)

    pair_copies = []
    for dx in range(nx):
        other = lax.rem(x + dx, nx)
        pair_send[dx] = dot(attended, wo_ref[:, columns(other * 2 + 1 - core)]).astype(BF16)
        copy = remote(pair_send.at[dx], pair_recv.at[dx], pair_ss.at[dx], pair_rs.at[dx], tp=sibling)
        copy.start()
        pair_copies.append(copy)
    for dx in range(nx):
        other = lax.rem(x + dx, nx)
        own_ref[dx] = dot(attended, wo_ref[:, columns(other * 2 + core)])
    part_copies = []
    for dx in sorted(range(1, nx), key=lambda d: -min(d, nx - d)):
        other = lax.rem(x + dx, nx)
        pair_copies[dx].wait()
        part_send[dx] = (own_ref[dx] + pair_recv[dx].astype(F32)).astype(BF16)
        copy = remote(
            part_send.at[dx], part_recv.at[dx], part_ss.at[dx], part_rs.at[dx], tp=other * 2 + core
        )
        copy.start()
        part_copies.append(copy)
    pair_copies[0].wait()
    projected = own_ref[0] + pair_recv[0].astype(F32)
    for copy in part_copies:
        copy.wait()
    for dx in range(1, nx):
        projected = projected + part_recv[dx].astype(F32)
    gated = (gating * projected).astype(BF16)

    back_send[...] = dot(spread, gated).astype(BF16)
    exchange(back_send, back_recv, back_ss, back_rs)
    exchange_wait(back_send, back_recv, back_ss, back_rs)
    out_ref[...] = dot(undeal, back_recv[...]).astype(BF16)


def build(cfg, tokens, router, gain, w_query, w_key, w_value, w_out, counts, picked):
    ny, nz, nx = cfg["ny"], cfg["nz"], cfg["nx"]
    rows, chunk, blocks = cfg["rows"], cfg["chunk"], cfg["blocks"]
    ctx, tp = ny * nz, nx * 2
    feats = tokens.shape[1]
    cap = picked.shape[1]
    slots = ctx * chunk
    half = rows // 2
    width = feats * tp
    tile = ny * rows // blocks
    far = nz // 2
    extra = jnp.concatenate([gain[None], router[None], jnp.zeros((14, feats), BF16)], axis=0)
    vmem = pl.BlockSpec(memory_space=pltpu.VMEM)
    hbm = pl.BlockSpec(memory_space=pl.ANY)
    dma = pltpu.SemaphoreType.DMA
    return pl.pallas_call(
        functools.partial(kernel, cfg),
        out_shape=jax.ShapeDtypeStruct((cap, feats), BF16),
        in_specs=[pl.BlockSpec(memory_space=pltpu.SMEM), vmem, vmem, vmem, hbm, hbm, hbm, hbm],
        out_specs=vmem,
        scratch_shapes=[
            pltpu.VMEM((width, feats), BF16),
            pltpu.VMEM((width, feats), BF16),
            pltpu.VMEM((width, feats), BF16),
            pltpu.VMEM((feats, width), BF16),
            pltpu.VMEM((slots, feats), BF16),
            pltpu.VMEM((slots, feats), BF16),
            pltpu.VMEM((tp, rows + 16, feats), BF16),
            pltpu.VMEM((rows, width), BF16),
            pltpu.VMEM((ny, rows, 2 * HD), BF16),
            pltpu.VMEM((nz, ny, rows, 2 * HD), BF16),
            pltpu.VMEM((ny, half, 2 * HD), BF16),
            pltpu.VMEM((ny, half, 2 * HD), BF16),
            pltpu.VMEM((ny, rows, 2 * HD), BF16),
            pltpu.VMEM((blocks, tile, 1), F32),
            pltpu.VMEM((blocks, tile, 1), F32),
            pltpu.VMEM((blocks, tile, 2 * HD), F32),
            pltpu.VMEM((ny, half, 2 * HD), BF16),
            pltpu.VMEM((ny, half, 2 * HD), BF16),
            pltpu.VMEM((nx, rows, feats), BF16),
            pltpu.VMEM((nx, rows, feats), BF16),
            pltpu.VMEM((nx, rows, feats), F32),
            pltpu.VMEM((nx, rows, feats), BF16),
            pltpu.VMEM((nx, rows, feats), BF16),
            pltpu.VMEM((slots, feats), BF16),
            pltpu.VMEM((slots, feats), BF16),
            dma((4,)),
            dma((ctx,)),
            dma((ctx,)),
            dma((2 * nx,)),
            dma((tp,)),
            dma((ny,)),
            dma((ny,)),
            dma((ny,)),
            dma((ny,)),
            dma((far, ny)),
            dma((far, ny)),
            dma((far, ny)),
            dma((far, ny)),
            dma((ny,)),
            dma((ny,)),
            dma((nx,)),
            dma((nx,)),
            dma((nx,)),
            dma((nx,)),
            dma((ctx,)),
            dma((ctx,)),
        ],
        compiler_params=pltpu.CompilerParams(
            collective_id=0, has_side_effects=True, vmem_limit_bytes=48 * 1024 * 1024
        ),
    )(counts, picked, tokens, extra, w_query, w_key, w_value, w_out)


def solution(mesh, nz=8, selected=6144, cap=384, blocks=3):
    ctx, tp = mesh.shape["ctx"], mesh.shape["tp"]
    per = -(-cap // ctx)
    cfg = {
        "ny": ctx // nz,
        "nz": nz,
        "nx": tp // 2,
        "rows": selected // ctx,
        "chunk": -(-per // 16) * 16,
        "blocks": blocks,
    }
    return jax.shard_map(
        functools.partial(build, cfg),
        mesh=mesh,
        in_specs=(
            P("ctx", "tp"),
            P("tp"),
            P("tp"),
            P(None, "tp"),
            P(None, "tp"),
            P(None, "tp"),
            P("tp", None),
            P(),
            P(),
        ),
        out_specs=P("ctx", "tp"),
        check_vma=False,
    )
```

```python
import functools
import math

import jax
import jax.numpy as jnp
from jax import lax
from jax.experimental import pallas as pl
from jax.experimental.pallas import tpu as pltpu
from jax.sharding import PartitionSpec as P

HD = 64
EPSILON = 1e-05
NEG_FILL = -1e30
MESH = pl.DeviceIdType.MESH
BF16 = jnp.bfloat16
F32 = jnp.float32
I32 = jnp.int32
VMEM_BYTES = 60 * 1024 * 1024


def iota(shape, dim):
    return lax.broadcasted_iota(I32, shape, dim)


def one_hot(mask):
    return jnp.where(mask, 1.0, 0.0).astype(BF16)


def dot(a, b):
    return jnp.dot(a, b, preferred_element_type=F32)


def dot_t(a, b):
    return lax.dot_general(a, b, (((1,), (1,)), ((), ())), preferred_element_type=F32)


def remote(src, dst, send, recv, **where):
    return pltpu.make_async_remote_copy(
        src_ref=src, dst_ref=dst, send_sem=send, recv_sem=recv, device_id=where, device_id_type=MESH
    )


class RingGather:
    def __init__(self, n, pos, core, view, ss, rs, device, sibling, parts=2):
        self.n, self.pos, self.core, self.view, self.ss, self.rs = n, pos, core, view, ss, rs
        self.device, self.sibling, self.parts = device, sibling, parts
        self.sent = []

    def at(self, step):
        return lax.rem(self.pos + step + self.n, self.n)

    def copy(self, pos, which, part, target):
        view = self.view(pos, which, part)
        return remote(view, view, self.ss.at[len(self.sent)], self.rs.at[pos, which, part], **target)

    def send(self, pos, part, target):
        copy = self.copy(pos, self.core, part, target)
        copy.start()
        self.sent.append(copy)

    def wait(self, pos, which, part):
        view = self.view(pos, which, part)
        remote(view, view, self.ss.at[0], self.rs.at[pos, which, part], **self.sibling).wait_recv()

    def start(self):
        right, left = self.device(self.at(1)), self.device(self.at(-1))
        parts = range(self.parts)
        for part in parts:
            if self.n > 1:
                self.send(self.pos, part, right)
            if self.n > 2:
                self.send(self.pos, self.parts - 1 - part, left)
        for part in parts:
            self.send(self.pos, part, self.sibling)

    def near(self):
        if self.n == 1:
            return
        right, left = self.device(self.at(1)), self.device(self.at(-1))
        for turn in range(self.parts):
            for step in (-1, 1) if self.n > 2 else (-1,):
                part = turn if step == -1 else self.parts - 1 - turn
                self.wait(self.at(step), self.core, part)
                if self.n > 2 and (turn == 0 and self.parts == 2 or self.parts == 1 and step == -1):
                    self.send(self.at(step), part, right if step == -1 else left)
                self.send(self.at(step), part, self.sibling)

    def far(self):
        if self.n > 2:
            for part in range(self.parts):
                self.wait(self.at(2), self.core, part)
                self.send(self.at(2), part, self.sibling)

    def from_sibling(self, pos):
        for part in range(self.parts):
            self.wait(pos, 1 - self.core, part)

    def finish(self):
        for copy in self.sent:
            copy.wait_send()


class Gather:
    def __init__(self, n, pos, core, view, ss, rs, device, sibling):
        self.n, self.pos, self.core, self.view, self.ss, self.rs = n, pos, core, view, ss, rs
        self.device, self.sibling = device, sibling
        self.sent = []

    def at(self, step):
        return lax.rem(self.pos + step, self.n)

    def copy(self, pos, which, slot, target):
        view = self.view(pos, which)
        return remote(view, view, self.ss.at[slot], self.rs.at[pos, which], **target)

    def send(self, pos, target):
        copy = self.copy(pos, self.core, len(self.sent), target)
        copy.start()
        self.sent.append(copy)

    def steps(self):
        return sorted(range(1, self.n), key=lambda d: min(d, self.n - d))

    def start(self):
        self.send(self.pos, self.sibling)
        for step in self.steps():
            self.send(self.pos, self.device(self.at(step)))

    def pass_on(self, step):
        self.copy(self.at(step), self.core, 0, self.sibling).wait_recv()
        self.send(self.at(step), self.sibling)

    def from_sibling(self, pos):
        self.copy(pos, 1 - self.core, 0, self.sibling).wait_recv()

    def finish(self):
        for copy in self.sent:
            copy.wait_send()


def kernel(
    cfg,
    counts_ref,
    gain_ref,
    router_ref,
    picked_hbm,
    tokens_hbm,
    wq_hbm,
    wk_hbm,
    wv_hbm,
    wo_hbm,
    out_ref,
    picked_ref,
    tokens_ref,
    wq_ref,
    wk_ref,
    wv_ref,
    wo_ref,
    row_send,
    row_recv,
    gathered,
    normed_ref,
    kv_send,
    kv_ref,
    q_send,
    q_recv,
    q_ref,
    value_ref,
    max_ref,
    acc_ref,
    att_send,
    att_recv,
    pair_send,
    pair_recv,
    own_ref,
    part_send,
    part_recv,
    back_send,
    back_recv,
    w_sem,
    row_ss,
    row_rs,
    gat_ss,
    gat_rs,
    kvz_ss,
    kvz_rs,
    qz_ss,
    qz_rs,
    kvy_ss,
    kvy_rs,
    att_ss,
    att_rs,
    pair_ss,
    pair_rs,
    part_ss,
    part_rs,
    back_ss,
    back_rs,
):
    ny, nz, nx = cfg["ny"], cfg["nz"], cfg["nx"]
    rows, chunk, blocks = cfg["rows"], cfg["chunk"], cfg["blocks"]
    ctx, tp = ny * nz, nx * 2
    seq, feats = tokens_ref.shape
    cap = picked_ref.shape[1]
    slots = ctx * chunk
    shift = chunk.bit_length() - 1
    half = rows // 2
    width = feats * tp
    heads = feats // HD
    zs = nz // 2

    loads = [
        pltpu.make_async_copy(src, dst, w_sem.at[i])
        for i, (src, dst) in enumerate(
            (
                (picked_hbm, picked_ref),
                (tokens_hbm, tokens_ref),
                (wk_hbm, wk_ref),
                (wv_hbm, wv_ref),
                (wq_hbm, wq_ref),
                (wo_hbm, wo_ref),
            )
        )
    ]
    for copy in loads:
        copy.start()

    c = lax.axis_index("ctx")
    t = lax.axis_index("tp")
    y, z = c // nz, lax.rem(c, nz)
    x, core = t // 2, lax.rem(t, 2)
    sibling = x * 2 + 1 - core

    barrier = pltpu.get_barrier_semaphore()

    def greet(i, _):
        pl.semaphore_signal(
            barrier, inc=1, device_id={"ctx": lax.rem(c + i, ctx)}, device_id_type=MESH
        )
        return 0

    lax.fori_loop(1, ctx, greet, 0)
    for dx in range(1, nx):
        pl.semaphore_signal(
            barrier,
            inc=1,
            device_id={"tp": lax.rem(x + dx, nx) * 2 + core},
            device_id_type=MESH,
        )
    pl.semaphore_signal(barrier, inc=1, device_id={"tp": sibling}, device_id_type=MESH)
    for dz in range(1, nz):
        pl.semaphore_signal(
            barrier,
            inc=1,
            device_id={"ctx": y * nz + lax.rem(z + dz, nz), "tp": sibling},
            device_id_type=MESH,
        )

    own_count = counts_ref[c]
    own_offset = jnp.int32(0)
    for i in range(ctx):
        own_offset = own_offset + jnp.where(i < c, counts_ref[i], 0)
    loads[0].wait()
    place_row = picked_ref[pl.ds(c, 1), :] - c * seq
    place_col = jnp.broadcast_to(place_row, (8, cap)).T[:, :1]
    live_row = iota((1, cap), 1) < own_count
    live_col = iota((cap, 1), 0) < own_count
    before_row = jnp.where(live_col & (place_col < place_row), 1.0, 0.0)
    order_row = jnp.where(live_row, jnp.sum(before_row, axis=0, keepdims=True).astype(I32), -1)

    def wanted(index):
        dest, number = index >> shift, index & (chunk - 1)
        return ((dest - own_offset) & (ctx - 1)) + ctx * number

    deal = one_hot(wanted(iota((slots, 1), 0)) == order_row)
    pick = one_hot(place_col == iota((cap, seq), 1))
    loads[1].wait()
    picked_rows = dot(pick, tokens_ref[...]).astype(BF16)
    row_send[...] = dot(deal, picked_rows).astype(BF16)

    pl.semaphore_wait(barrier, ctx - 1 + nx + nz - 1)

    def span(i):
        return pl.ds(pl.multiple_of(i * chunk, chunk), chunk)

    def exchange(send_ref, recv_ref, ss, rs):
        def begin(i, _):
            d = lax.rem(c + i, ctx)
            remote(
                send_ref.at[span(d)], recv_ref.at[span(c)], ss.at[d], rs.at[c], ctx=d
            ).start()
            return 0

        lax.fori_loop(1, ctx, begin, 0)
        recv_ref[span(c), :] = send_ref[span(c), :]

    def exchange_wait(send_ref, recv_ref, ss, rs):
        def end(i, _):
            d = lax.rem(c + i, ctx)
            remote(send_ref.at[span(d)], recv_ref.at[span(d)], ss.at[d], rs.at[d], ctx=d).wait()
            return 0

        lax.fori_loop(1, ctx, end, 0)

    exchange(row_send, row_recv, row_ss, row_rs)

    source = iota((8, slots), 1) >> shift
    offset_of = jnp.zeros((8, slots), I32)
    count_of = jnp.zeros((8, slots), I32)
    for i in range(ctx):
        count = counts_ref[i]
        offset_of = offset_of + jnp.where(source > i, count, 0)
        count_of = count_of + jnp.where(source == i, count, 0)
    number = ((c - offset_of) & (ctx - 1)) + ctx * (iota((8, slots), 1) & (chunk - 1))
    local_index = jnp.where(number < count_of, (offset_of + number - c) >> (ctx.bit_length() - 1), -1)
    compact = one_hot(local_index[:1] == iota((rows, slots), 0))
    spread_index = local_index.T[:, :1]
    spread = one_hot(spread_index == iota((slots, rows), 1))

    before_col = jnp.where(live_row & (place_row < place_col), 1.0, 0.0)
    order_col = jnp.where(live_col, jnp.sum(before_col, axis=1, keepdims=True).astype(I32), -1)
    undeal = one_hot(order_col == wanted(iota((1, slots), 1)))

    exchange_wait(row_send, row_recv, row_ss, row_rs)

    gathered[t, pl.ds(0, rows), :] = dot(compact, row_recv[...]).astype(BF16)
    params = jnp.concatenate(
        [
            gain_ref[...].astype(F32).reshape(1, feats),
            router_ref[...].astype(F32).reshape(1, feats),
            jnp.zeros((14, feats), F32),
        ],
        axis=0,
    )
    gathered[t, pl.ds(rows, 16), :] = params.astype(BF16)

    features = Gather(
        nx,
        x,
        core,
        lambda pos, which: gathered.at[pos * 2 + which],
        gat_ss,
        gat_rs,
        lambda pos: {"tp": pos * 2 + core},
        {"tp": sibling},
    )
    features.start()
    for step in features.steps():
        features.pass_on(step)
    for pos in range(nx):
        features.from_sibling(pos)
    features.finish()

    squares = jnp.zeros((rows, feats), F32)
    routes = jnp.zeros((rows, feats), F32)
    for b in range(tp):
        wide = gathered[b, pl.ds(0, rows), :].astype(F32)
        params = gathered[b, pl.ds(rows, 16), :].astype(F32)
        squares = squares + wide * wide
        routes = routes + wide * params[1:2]
    scale = lax.rsqrt(jnp.sum(squares, axis=1, keepdims=True) / width + EPSILON)
    gating = 1.0 / (1.0 + jnp.exp(-jnp.sum(routes, axis=1, keepdims=True)))
    for b in range(tp):
        wide = gathered[b, pl.ds(0, rows), :].astype(F32)
        params = gathered[b, pl.ds(rows, 16), :].astype(F32)
        normed_ref[:, pl.ds(b * feats, feats)] = (wide * scale * params[0:1]).astype(BF16)

    for copy in loads[2:]:
        copy.wait()
    normed = normed_ref[...]
    keys = dot(normed, wk_ref[...]).astype(BF16)
    values = dot(normed, wv_ref[...]).astype(BF16)
    for h in range(heads):
        cols = slice(h * HD, (h + 1) * HD)
        kv_send[h] = jnp.concatenate([keys[:, cols], values[:, cols]], axis=1)

    zi, parity = z // 2, lax.rem(z, 2)
    head_core = z // heads

    def to_head(h, send_ref, target, ss, rs):
        return remote(
            send_ref.at[h],
            target(zi, parity),
            ss.at[h],
            rs.at[zi],
            ctx=y * nz + heads * core + h,
            tp=x * 2 + parity,
        )

    def stays(h):
        return (heads * core + h == z) & (parity == core)

    def from_head(source, send_ref, target, ss, rs):
        return remote(
            send_ref.at[0],
            target(source, core),
            ss.at[0],
            rs.at[source],
            ctx=y * nz + source * 2 + core,
            tp=x * 2 + head_core,
        )

    def came(source):
        return (source * 2 + core == z) & (head_core == core)

    kv_target = lambda source, which: kv_ref.at[y, which, source]
    q_target = lambda source, which: q_recv.at[source]

    def deal_heads(send_ref, target, ss, rs):
        for h in range(heads):

            @pl.when(stays(h))
            def _():
                target(zi, core)[...] = send_ref[h]

            @pl.when(jnp.logical_not(stays(h)))
            def _():
                to_head(h, send_ref, target, ss, rs).start()

    def deal_heads_wait(send_ref, target, ss, rs):
        for source in range(zs):

            @pl.when(jnp.logical_not(came(source)))
            def _():
                from_head(source, send_ref, target, ss, rs).wait_recv()

    def deal_heads_sent(send_ref, target, ss, rs):
        for h in range(heads):

            @pl.when(jnp.logical_not(stays(h)))
            def _():
                to_head(h, send_ref, target, ss, rs).wait_send()

    deal_heads(kv_send, kv_target, kvz_ss, kvz_rs)

    queries = (dot(normed, wq_ref[...]).astype(BF16).astype(F32) * (1.0 / math.sqrt(HD))).astype(BF16)
    for h in range(heads):
        cols = slice(h * HD, (h + 1) * HD)
        q_send[h] = jnp.concatenate([queries[:half, cols], queries[half:, cols]], axis=1)
    deal_heads(q_send, q_target, qz_ss, qz_rs)

    def kv_view(pos, which, part):
        split = (zs + 1) // 2
        return kv_ref.at[pos, which, pl.ds(0, split) if part == 0 else pl.ds(split, zs - split)]

    blocks_kv = RingGather(
        ny,
        y,
        core,
        kv_view,
        kvy_ss,
        kvy_rs,
        lambda pos: {"ctx": pos * nz + z},
        {"tp": sibling},
        parts=2 if zs > 1 else 1,
    )
    deal_heads_wait(kv_send, kv_target, kvz_ss, kvz_rs)
    blocks_kv.start()
    deal_heads_wait(q_send, q_target, qz_ss, qz_rs)

    zeros = jnp.zeros((half, HD), BF16)
    for source in range(zs):
        packed = q_recv[source]
        q_ref[source, pl.ds(0, half), :] = jnp.concatenate([packed[:, :HD], zeros], axis=1)
        q_ref[source, pl.ds(half, half), :] = jnp.concatenate([packed[:, HD:], zeros], axis=1)

    size = rows // blocks
    tile = zs * size
    tile_row = iota((tile, 1), 0)
    tile_col = iota((1, tile), 1)
    query_key = lax.rem(tile_row, size) * ctx + y * nz + (tile_row // size) * 2 + core
    key_base = lax.rem(tile_col, size) * ctx + (tile_col // size) * 2
    value_lane = iota((1, 1, 2 * HD), 2) >= HD

    def attend(pairs, first):
        allowed = []
        for i, (pos, which) in enumerate(pairs):
            value_ref[i] = jnp.where(value_lane, kv_ref[pos, which], jnp.ones((), BF16))
            allowed.append(key_base + (pos * nz + which) <= query_key)
        for b in range(blocks):
            q = q_ref[:, pl.ds(b * size, size), :].reshape(tile, 2 * HD)
            scores, operands = [], []
            for i, (pos, which) in enumerate(pairs):
                now = pl.ds(b * size, size)
                near = kv_ref[pos, which, :, now, :].reshape(tile, 2 * HD)
                scores.append(jnp.where(allowed[i], dot_t(q, near), NEG_FILL))
                operands.append(value_ref[i, :, now, :].reshape(tile, 2 * HD))
                if b:
                    before = pl.ds(0, b * size)
                    past = kv_ref[pos, which, :, before, :].reshape(b * tile, 2 * HD)
                    scores.append(dot_t(q, past))
                    operands.append(value_ref[i, :, before, :].reshape(b * tile, 2 * HD))
            peak = None if first else max_ref[b]
            for score in scores:
                top = jnp.max(score, axis=1, keepdims=True)
                peak = top if peak is None else jnp.maximum(peak, top)
            product = None if first else acc_ref[b] * jnp.exp(max_ref[b] - peak)
            for score, operand in zip(scores, operands):
                term = dot(jnp.exp(score - peak).astype(BF16), operand)
                product = term if product is None else product + term
            max_ref[b] = peak
            acc_ref[b] = product

    blocks_kv.from_sibling(y)
    attend([(y, core), (y, 1 - core)], True)
    blocks_kv.near()
    near_by = [lax.rem(y + d, ny) for d in range(1, ny, 2)]
    far_off = [lax.rem(y + d, ny) for d in range(2, ny, 2)]
    if near_by:
        attend([(pos, core) for pos in near_by], False)
        blocks_kv.far()
        for pos in near_by:
            blocks_kv.from_sibling(pos)
        attend([(pos, 1 - core) for pos in near_by], False)
        for pos in far_off:
            blocks_kv.from_sibling(pos)
            attend([(pos, core), (pos, 1 - core)], False)
    blocks_kv.finish()
    deal_heads_sent(kv_send, kv_target, kvz_ss, kvz_rs)
    deal_heads_sent(q_send, q_target, qz_ss, qz_rs)

    for b in range(blocks):
        sums = acc_ref[b]
        result = sums[:, HD:] / sums[:, :HD]
        value_ref[0, :, pl.ds(b * size, size), :HD] = result.astype(BF16).reshape(zs, size, HD)
    for source in range(zs):
        att_send[source] = jnp.concatenate(
            [value_ref[0, source, pl.ds(0, half), :][:, :HD], value_ref[0, source, pl.ds(half, half), :][:, :HD]],
            axis=1,
        )
    own_head = lax.rem(z, heads)
    for source in range(zs):

        @pl.when(came(source))
        def _():
            att_recv[own_head] = att_send[source]

        @pl.when(jnp.logical_not(came(source)))
        def _():
            remote(
                att_send.at[source],
                att_recv.at[own_head],
                att_ss.at[source],
                att_rs.at[own_head],
                ctx=y * nz + source * 2 + core,
                tp=x * 2 + head_core,
            ).start()

    for h in range(heads):

        @pl.when(jnp.logical_not(stays(h)))
        def _():
            remote(
                att_send.at[0],
                att_recv.at[h],
                att_ss.at[0],
                att_rs.at[h],
                ctx=y * nz + heads * core + h,
                tp=x * 2 + parity,
            ).wait_recv()

    joined = [att_recv[h] for h in range(heads)]
    attended = jnp.concatenate(
        [
            jnp.concatenate([packed[:, :HD] for packed in joined], axis=1),
            jnp.concatenate([packed[:, HD:] for packed in joined], axis=1),
        ],
        axis=0,
    )

    def columns(index):
        return pl.ds(pl.multiple_of(index * feats, feats), feats)

    pair_order = [2, 1, 3, 0] if nx == 4 else [1, 0] if nx == 2 else [0]
    pair_copies = [None] * nx
    for dx in pair_order:
        other = lax.rem(x + dx, nx)
        pair_send[dx] = dot(attended, wo_ref[:, columns(other * 2 + 1 - core)]).astype(BF16)
        copy = remote(pair_send.at[dx], pair_recv.at[dx], pair_ss.at[dx], pair_rs.at[dx], tp=sibling)
        copy.start()
        pair_copies[dx] = copy
    for dx in pair_order:
        other = lax.rem(x + dx, nx)
        own_ref[dx] = dot(attended, wo_ref[:, columns(other * 2 + core)])
    part_copies = []
    for dx in pair_order[:-1]:
        other = lax.rem(x + dx, nx)
        pair_copies[dx].wait()
        part_send[dx] = (own_ref[dx] + pair_recv[dx].astype(F32)).astype(BF16)
        copy = remote(
            part_send.at[dx], part_recv.at[dx], part_ss.at[dx], part_rs.at[dx], tp=other * 2 + core
        )
        copy.start()
        part_copies.append(copy)
    pair_copies[0].wait()
    projected = own_ref[0] + pair_recv[0].astype(F32)
    for copy in reversed(part_copies):
        copy.wait()
    for dx in range(1, nx):
        projected = projected + part_recv[dx].astype(F32)
    gated = (gating * projected).astype(BF16)

    for source in range(zs):

        @pl.when(jnp.logical_not(came(source)))
        def _():
            remote(
                att_send.at[source],
                att_recv.at[own_head],
                att_ss.at[source],
                att_rs.at[own_head],
                ctx=y * nz + source * 2 + core,
                tp=x * 2 + head_core,
            ).wait_send()

    back_send[...] = dot(spread, gated).astype(BF16)
    exchange(back_send, back_recv, back_ss, back_rs)
    exchange_wait(back_send, back_recv, back_ss, back_rs)
    out_ref[...] = dot(undeal, back_recv[...]).astype(BF16)


def build(cfg, tokens, router, gain, w_query, w_key, w_value, w_out, counts, picked):
    ny, nz, nx = cfg["ny"], cfg["nz"], cfg["nx"]
    rows, chunk, blocks = cfg["rows"], cfg["chunk"], cfg["blocks"]
    ctx, tp = ny * nz, nx * 2
    feats = tokens.shape[1]
    cap = picked.shape[1]
    slots = ctx * chunk
    half = rows // 2
    width = feats * tp
    heads = feats // HD
    zs = nz // 2
    tile = zs * rows // blocks
    vmem = pl.BlockSpec(memory_space=pltpu.VMEM)
    hbm = pl.BlockSpec(memory_space=pltpu.HBM)
    dma = pltpu.SemaphoreType.DMA
    return pl.pallas_call(
        functools.partial(kernel, cfg),
        out_shape=jax.ShapeDtypeStruct((cap, feats), BF16),
        in_specs=[pl.BlockSpec(memory_space=pltpu.SMEM)] + [vmem] * 2 + [hbm] * 6,
        out_specs=vmem,
        scratch_shapes=[
            pltpu.VMEM(picked.shape, I32),
            pltpu.VMEM(tokens.shape, BF16),
            pltpu.VMEM((width, feats), BF16),
            pltpu.VMEM((width, feats), BF16),
            pltpu.VMEM((width, feats), BF16),
            pltpu.VMEM((feats, width), BF16),
            pltpu.VMEM((slots, feats), BF16),
            pltpu.VMEM((slots, feats), BF16),
            pltpu.VMEM((tp, rows + 16, feats), BF16),
            pltpu.VMEM((rows, width), BF16),
            pltpu.VMEM((heads, rows, 2 * HD), BF16),
            pltpu.VMEM((ny, 2, zs, rows, 2 * HD), BF16),
            pltpu.VMEM((heads, half, 2 * HD), BF16),
            pltpu.VMEM((zs, half, 2 * HD), BF16),
            pltpu.VMEM((zs, rows, 2 * HD), BF16),
            pltpu.VMEM((2, zs, rows, 2 * HD), BF16),
            pltpu.VMEM((blocks, tile, 1), F32),
            pltpu.VMEM((blocks, tile, 2 * HD), F32),
            pltpu.VMEM((zs, half, 2 * HD), BF16),
            pltpu.VMEM((heads, half, 2 * HD), BF16),
            pltpu.VMEM((nx, rows, feats), BF16),
            pltpu.VMEM((nx, rows, feats), BF16),
            pltpu.VMEM((nx, rows, feats), F32),
            pltpu.VMEM((nx, rows, feats), BF16),
            pltpu.VMEM((nx, rows, feats), BF16),
            pltpu.VMEM((slots, feats), BF16),
            pltpu.VMEM((slots, feats), BF16),
            dma((6,)),
            dma((ctx,)),
            dma((ctx,)),
            dma((2 * nx,)),
            dma((nx, 2)),
            dma((heads,)),
            dma((zs,)),
            dma((heads,)),
            dma((zs,)),
            dma((4 * ny + 4,)),
            dma((ny, 2, 2)),
            dma((zs,)),
            dma((heads,)),
            dma((nx,)),
            dma((nx,)),
            dma((nx,)),
            dma((nx,)),
            dma((ctx,)),
            dma((ctx,)),
        ],
        compiler_params=pltpu.CompilerParams(
            collective_id=0, has_side_effects=True, vmem_limit_bytes=VMEM_BYTES
        ),
    )(counts, gain, router, picked, tokens, w_query, w_key, w_value, w_out)


def solution(mesh, nz=8, selected=6144, cap=384, blocks=3):
    ctx, tp = mesh.shape["ctx"], mesh.shape["tp"]
    per = -(-cap // ctx)
    cfg = {
        "ny": ctx // nz,
        "nz": nz,
        "nx": tp // 2,
        "rows": selected // ctx,
        "chunk": -(-per // 16) * 16,
        "blocks": blocks,
    }
    return jax.shard_map(
        functools.partial(build, cfg),
        mesh=mesh,
        in_specs=(
            P("ctx", "tp"),
            P("tp"),
            P("tp"),
            P(None, "tp"),
            P(None, "tp"),
            P(None, "tp"),
            P("tp", None),
            P(),
            P(),
        ),
        out_specs=P("ctx", "tp"),
        check_vma=False,
    )
```

```python
import functools
import math

import jax
import jax.numpy as jnp
from jax import lax
from jax.experimental import pallas as pl
from jax.experimental.pallas import tpu as pltpu
from jax.sharding import PartitionSpec as P

HD = 64
EPSILON = 1e-05
NEG_FILL = -1e30
MESH = pl.DeviceIdType.MESH
BF16 = jnp.bfloat16
F32 = jnp.float32
I32 = jnp.int32
VMEM_BYTES = 60 * 1024 * 1024


def iota(shape, dim):
    return lax.broadcasted_iota(I32, shape, dim)


def one_hot(mask):
    return jnp.where(mask, 1.0, 0.0).astype(BF16)


def dot(a, b):
    return jnp.dot(a, b, preferred_element_type=F32)


def dot_t(a, b):
    return lax.dot_general(a, b, (((1,), (1,)), ((), ())), preferred_element_type=F32)


def remote(src, dst, send, recv, **where):
    return pltpu.make_async_remote_copy(
        src_ref=src, dst_ref=dst, send_sem=send, recv_sem=recv, device_id=where, device_id_type=MESH
    )


class RingGather:
    def __init__(self, n, pos, core, view, ss, rs, device, sibling, parts=2):
        self.n, self.pos, self.core, self.view, self.ss, self.rs = n, pos, core, view, ss, rs
        self.device, self.sibling, self.parts = device, sibling, parts
        self.sent = []

    def at(self, step):
        return lax.rem(self.pos + step + self.n, self.n)

    def copy(self, pos, which, part, target):
        view = self.view(pos, which, part)
        return remote(view, view, self.ss(len(self.sent)), self.rs(pos, which, part), **target)

    def send(self, pos, part, target):
        copy = self.copy(pos, self.core, part, target)
        copy.start()
        self.sent.append(copy)

    def wait(self, pos, which, part):
        view = self.view(pos, which, part)
        remote(view, view, self.ss(0), self.rs(pos, which, part), **self.sibling).wait_recv()

    def start(self):
        right, left = self.device(self.at(1)), self.device(self.at(-1))
        parts = range(self.parts)
        for part in parts:
            if self.n > 1:
                self.send(self.pos, part, right)
            if self.n > 2:
                self.send(self.pos, self.parts - 1 - part, left)
        for part in parts:
            self.send(self.pos, part, self.sibling)

    def near(self):
        if self.n == 1:
            return
        right, left = self.device(self.at(1)), self.device(self.at(-1))
        for turn in range(self.parts):
            for step in (-1, 1) if self.n > 2 else (-1,):
                part = turn if step == -1 else self.parts - 1 - turn
                self.wait(self.at(step), self.core, part)
                if self.n > 2 and (turn == 0 and self.parts == 2 or self.parts == 1 and step == -1):
                    self.send(self.at(step), part, right if step == -1 else left)
                self.send(self.at(step), part, self.sibling)

    def far(self):
        if self.n > 2:
            for part in range(self.parts):
                self.wait(self.at(2), self.core, part)
                self.send(self.at(2), part, self.sibling)

    def from_sibling(self, pos):
        for part in range(self.parts):
            self.wait(pos, 1 - self.core, part)

    def finish(self):
        for copy in self.sent:
            copy.wait_send()


class Gather:
    def __init__(self, n, pos, core, view, ss, rs, device, sibling):
        self.n, self.pos, self.core, self.view, self.ss, self.rs = n, pos, core, view, ss, rs
        self.device, self.sibling = device, sibling
        self.sent = []

    def at(self, step):
        return lax.rem(self.pos + step, self.n)

    def copy(self, pos, which, slot, target):
        view = self.view(pos, which)
        return remote(view, view, self.ss(slot), self.rs(pos, which), **target)

    def send(self, pos, target):
        copy = self.copy(pos, self.core, len(self.sent), target)
        copy.start()
        self.sent.append(copy)

    def steps(self):
        return sorted(range(1, self.n), key=lambda d: min(d, self.n - d))

    def start(self):
        self.send(self.pos, self.sibling)
        for step in self.steps():
            self.send(self.pos, self.device(self.at(step)))

    def pass_on(self, step):
        self.copy(self.at(step), self.core, 0, self.sibling).wait_recv()
        self.send(self.at(step), self.sibling)

    def from_sibling(self, pos):
        self.copy(pos, 1 - self.core, 0, self.sibling).wait_recv()

    def finish(self):
        for copy in self.sent:
            copy.wait_send()


def kernel(
    cfg,
    counts_ref,
    gain_ref,
    router_ref,
    picked_hbm,
    tokens_hbm,
    wq_hbm,
    wk_hbm,
    wv_hbm,
    wo_hbm,
    out_ref,
    picked_ref,
    tokens_ref,
    wq_ref,
    wk_ref,
    wv_ref,
    wo_ref,
    row_send,
    row_recv,
    gathered,
    normed_ref,
    kv_send,
    kv_ref,
    q_send,
    q_recv,
    q_ref,
    value_ref,
    max_ref,
    acc_ref,
    done_ref,
    gated_ref,
    att_send,
    att_recv,
    pair_send,
    pair_recv,
    own_ref,
    part_send,
    part_recv,
    back_send,
    back_recv,
    w_sem,
    row_ss,
    row_rs,
    gat_ss,
    gat_rs,
    kvz_ss,
    kvz_rs,
    qz_ss,
    qz_rs,
    kvy_ss,
    kvy_rs,
    att_ss,
    att_rs,
    pair_ss,
    pair_rs,
    part_ss,
    part_rs,
    back_ss,
    back_rs,
):
    ny, nz, nx = cfg["ny"], cfg["nz"], cfg["nx"]
    rows, chunk, blocks = cfg["rows"], cfg["chunk"], cfg["blocks"]
    ctx, tp = ny * nz, nx * 2
    seq, feats = tokens_ref.shape
    cap = picked_ref.shape[1]
    slots = ctx * chunk
    shift = chunk.bit_length() - 1
    half = rows // 2
    quarter = half // 2
    width = feats * tp
    heads = feats // HD
    zs = nz // 2

    loads = [
        pltpu.make_async_copy(src, dst, w_sem.at[i])
        for i, (src, dst) in enumerate(
            (
                (picked_hbm, picked_ref),
                (tokens_hbm, tokens_ref),
                (wk_hbm, wk_ref),
                (wv_hbm, wv_ref),
                (wq_hbm, wq_ref),
                (wo_hbm, wo_ref),
            )
        )
    ]
    for copy in loads:
        copy.start()

    c = lax.axis_index("ctx")
    t = lax.axis_index("tp")
    y, z = c // nz, lax.rem(c, nz)
    x, core = t // 2, lax.rem(t, 2)
    sibling = x * 2 + 1 - core

    barrier = pltpu.get_barrier_semaphore()

    def greet(i, _):
        pl.semaphore_signal(
            barrier, inc=1, device_id={"ctx": lax.rem(c + i, ctx)}, device_id_type=MESH
        )
        return 0

    lax.fori_loop(1, ctx, greet, 0)
    for dx in range(1, nx):
        pl.semaphore_signal(
            barrier,
            inc=1,
            device_id={"tp": lax.rem(x + dx, nx) * 2 + core},
            device_id_type=MESH,
        )
    pl.semaphore_signal(barrier, inc=1, device_id={"tp": sibling}, device_id_type=MESH)
    for dz in range(1, nz):
        pl.semaphore_signal(
            barrier,
            inc=1,
            device_id={"ctx": y * nz + lax.rem(z + dz, nz), "tp": sibling},
            device_id_type=MESH,
        )

    own_count = counts_ref[c]
    own_offset = jnp.int32(0)
    for i in range(ctx):
        own_offset = own_offset + jnp.where(i < c, counts_ref[i], 0)
    loads[0].wait()
    place_row = picked_ref[pl.ds(c, 1), :] - c * seq
    place_col = jnp.broadcast_to(place_row, (8, cap)).T[:, :1]
    live_row = iota((1, cap), 1) < own_count
    live_col = iota((cap, 1), 0) < own_count
    before_row = jnp.where(live_col & (place_col < place_row), 1.0, 0.0)
    order_row = jnp.where(live_row, jnp.sum(before_row, axis=0, keepdims=True).astype(I32), -1)

    def wanted(index):
        dest, number = index >> shift, index & (chunk - 1)
        return ((dest - own_offset) & (ctx - 1)) + ctx * number

    deal = one_hot(wanted(iota((slots, 1), 0)) == order_row)
    pick = one_hot(place_col == iota((cap, seq), 1))
    loads[1].wait()
    picked_rows = dot(pick, tokens_ref[...]).astype(BF16)
    row_send[...] = dot(deal, picked_rows).astype(BF16)

    pl.semaphore_wait(barrier, ctx - 1 + nx + nz - 1)

    def span(i):
        return pl.ds(pl.multiple_of(i * chunk, chunk), chunk)

    def exchange(send_ref, recv_ref, ss, rs):
        def begin(i, _):
            d = lax.rem(c + i, ctx)
            remote(
                send_ref.at[span(d)], recv_ref.at[span(c)], ss.at[d], rs.at[c], ctx=d
            ).start()
            return 0

        lax.fori_loop(1, ctx, begin, 0)
        recv_ref[span(c), :] = send_ref[span(c), :]

    def exchange_wait(send_ref, recv_ref, ss, rs):
        def end(i, _):
            d = lax.rem(c + i, ctx)
            remote(send_ref.at[span(d)], recv_ref.at[span(d)], ss.at[d], rs.at[d], ctx=d).wait()
            return 0

        lax.fori_loop(1, ctx, end, 0)

    exchange(row_send, row_recv, row_ss, row_rs)

    source = iota((8, slots), 1) >> shift
    offset_of = jnp.zeros((8, slots), I32)
    count_of = jnp.zeros((8, slots), I32)
    for i in range(ctx):
        count = counts_ref[i]
        offset_of = offset_of + jnp.where(source > i, count, 0)
        count_of = count_of + jnp.where(source == i, count, 0)
    number = ((c - offset_of) & (ctx - 1)) + ctx * (iota((8, slots), 1) & (chunk - 1))
    local_index = jnp.where(number < count_of, (offset_of + number - c) >> (ctx.bit_length() - 1), -1)
    compact = one_hot(local_index[:1] == iota((rows, slots), 0))
    spread_index = local_index.T[:, :1]
    spread = one_hot(spread_index == iota((slots, rows), 1))

    before_col = jnp.where(live_row & (place_row < place_col), 1.0, 0.0)
    order_col = jnp.where(live_col, jnp.sum(before_col, axis=1, keepdims=True).astype(I32), -1)
    undeal = one_hot(order_col == wanted(iota((1, slots), 1)))

    exchange_wait(row_send, row_recv, row_ss, row_rs)

    packed_rows = dot(compact, row_recv[...]).astype(BF16)
    params = jnp.concatenate(
        [
            gain_ref[...].astype(F32).reshape(1, feats),
            router_ref[...].astype(F32).reshape(1, feats),
            jnp.zeros((14, feats), F32),
        ],
        axis=0,
    )
    gathered[0, t, pl.ds(0, half), :] = packed_rows[:half]
    gathered[0, t, pl.ds(half, 16), :] = params.astype(BF16)
    gathered[1, t, pl.ds(0, half), :] = packed_rows[half:]

    def feature_gather(p):
        height = half + 16 if p == 0 else half
        return Gather(
            nx,
            x,
            core,
            lambda pos, which: gathered.at[p, pos * 2 + which, pl.ds(0, height), :],
            lambda slot: gat_ss.at[p, slot],
            lambda pos, which: gat_rs.at[p, pos, which],
            lambda pos: {"tp": pos * 2 + core},
            {"tp": sibling},
        )

    features = [feature_gather(0), feature_gather(1)]
    features[0].start()
    features[1].start()

    zi, parity = z // 2, lax.rem(z, 2)
    head_core = z // heads
    own_head = lax.rem(z, heads)

    def stays(h):
        return (heads * core + h == z) & (parity == core)

    def came(source):
        return (source * 2 + core == z) & (head_core == core)

    def to_head(h, src, dst, ss, rs):
        return remote(src, dst, ss, rs, ctx=y * nz + heads * core + h, tp=x * 2 + parity)

    def to_source(source, src, dst, ss, rs):
        return remote(src, dst, ss, rs, ctx=y * nz + source * 2 + core, tp=x * 2 + head_core)

    def kv_at(p, source, which):
        return kv_ref.at[y, which, p, source]

    def q_at(p, source, which):
        return q_recv.at[p, source]

    def deal_heads(p, send_ref, target, ss, rs):
        for h in range(heads):

            @pl.when(stays(h))
            def _():
                target(p, zi, core)[...] = send_ref[p, h]

            @pl.when(jnp.logical_not(stays(h)))
            def _():
                to_head(h, send_ref.at[p, h], target(p, zi, parity), ss.at[p, h], rs.at[p, zi]).start()

    def deal_heads_wait(p, send_ref, target, ss, rs):
        for source in range(zs):

            @pl.when(jnp.logical_not(came(source)))
            def _():
                to_source(
                    source, send_ref.at[p, 0], target(p, source, core), ss.at[p, 0], rs.at[p, source]
                ).wait_recv()

    def deal_heads_sent(p, send_ref, target, ss, rs):
        for h in range(heads):

            @pl.when(jnp.logical_not(stays(h)))
            def _():
                to_head(h, send_ref.at[p, h], target(p, zi, parity), ss.at[p, h], rs.at[p, zi]).wait_send()

    def project(p):
        squares = jnp.zeros((half, feats), F32)
        routes = jnp.zeros((half, feats), F32)
        for b in range(tp):
            wide = gathered[p, b, pl.ds(0, half), :].astype(F32)
            params = gathered[0, b, pl.ds(half, 16), :].astype(F32)
            squares = squares + wide * wide
            routes = routes + wide * params[1:2]
        scale = lax.rsqrt(jnp.sum(squares, axis=1, keepdims=True) / width + EPSILON)
        for b in range(tp):
            wide = gathered[p, b, pl.ds(0, half), :].astype(F32)
            params = gathered[0, b, pl.ds(half, 16), :].astype(F32)
            normed_ref[p, :, pl.ds(b * feats, feats)] = (wide * scale * params[0:1]).astype(BF16)
        normed = normed_ref[p]
        keys = dot(normed, wk_ref[...]).astype(BF16)
        values = dot(normed, wv_ref[...]).astype(BF16)
        for h in range(heads):
            cols = slice(h * HD, (h + 1) * HD)
            kv_send[p, h] = jnp.concatenate([keys[:, cols], values[:, cols]], axis=1)
        deal_heads(p, kv_send, kv_at, kvz_ss, kvz_rs)
        queries = (dot(normed, wq_ref[...]).astype(BF16).astype(F32) * (1.0 / math.sqrt(HD))).astype(BF16)
        for h in range(heads):
            cols = slice(h * HD, (h + 1) * HD)
            q_send[p, h] = jnp.concatenate([queries[:quarter, cols], queries[quarter:, cols]], axis=1)
        deal_heads(p, q_send, q_at, qz_ss, qz_rs)
        return 1.0 / (1.0 + jnp.exp(-jnp.sum(routes, axis=1, keepdims=True)))

    def gather_end(p):
        for step in features[p].steps():
            features[p].pass_on(step)
        for pos in range(nx):
            features[p].from_sibling(pos)

    gather_end(0)
    for copy in loads[2:]:
        copy.wait()
    gating = [project(0)]
    gather_end(1)
    gating.append(project(1))

    kv_parts = 2 if zs > 1 else 1

    def kv_gather(p):
        split = (zs + 1) // 2
        return RingGather(
            ny,
            y,
            core,
            lambda pos, which, part: kv_ref.at[
                pos, which, p, pl.ds(0, split) if part == 0 else pl.ds(split, zs - split)
            ],
            lambda slot: kvy_ss.at[p, slot],
            lambda pos, which, part: kvy_rs.at[p, pos, which, part],
            lambda pos: {"ctx": pos * nz + z},
            {"tp": sibling},
            parts=kv_parts,
        )

    blocks_kv = [kv_gather(0), kv_gather(1)]
    size = half // blocks
    tile = zs * size
    tile_row = iota((tile, 1), 0)
    tile_col = iota((1, tile), 1)
    query_key = lax.rem(tile_row, size) * ctx + y * nz + (tile_row // size) * 2 + core
    key_base = lax.rem(tile_col, size) * ctx + (tile_col // size) * 2
    value_lane = iota((1, 1, 2 * HD), 2) >= HD
    zeros = jnp.zeros((quarter, HD), BF16)

    def queries_in(p):
        deal_heads_wait(p, q_send, q_at, qz_ss, qz_rs)
        for source in range(zs):
            packed = q_recv[p, source]
            q_ref[p, source, pl.ds(0, quarter), :] = jnp.concatenate([packed[:, :HD], zeros], axis=1)
            q_ref[p, source, pl.ds(quarter, quarter), :] = jnp.concatenate([packed[:, HD:], zeros], axis=1)

    def attend(p, pairs, first=False):
        allowed = []
        for pos, which in pairs:
            value_ref[pos, which, p] = jnp.where(value_lane, kv_ref[pos, which, p], jnp.ones((), BF16))
            allowed.append(key_base + (pos * nz + which) <= query_key)
        for b in range(blocks):
            now = pl.ds(b * size, size)
            q = q_ref[p, :, now, :].reshape(tile, 2 * HD)
            scores, operands = [], []
            for i, (pos, which) in enumerate(pairs):
                near = kv_ref[pos, which, p, :, now, :].reshape(tile, 2 * HD)
                scores.append(jnp.where(allowed[i], dot_t(q, near), NEG_FILL))
                operands.append(value_ref[pos, which, p, :, now, :].reshape(tile, 2 * HD))
                if b:
                    before = pl.ds(0, b * size)
                    past = kv_ref[pos, which, p, :, before, :].reshape(b * tile, 2 * HD)
                    scores.append(dot_t(q, past))
                    operands.append(value_ref[pos, which, p, :, before, :].reshape(b * tile, 2 * HD))
                if p:
                    scores.append(dot_t(q, kv_ref[pos, which, 0].reshape(zs * half, 2 * HD)))
                    operands.append(value_ref[pos, which, 0].reshape(zs * half, 2 * HD))
            peak = None if first else max_ref[p, b]
            for score in scores:
                top = jnp.max(score, axis=1, keepdims=True)
                peak = top if peak is None else jnp.maximum(peak, top)
            product = None if first else acc_ref[p, b] * jnp.exp(max_ref[p, b] - peak)
            for score, operand in zip(scores, operands):
                term = dot(jnp.exp(score - peak).astype(BF16), operand)
                product = term if product is None else product + term
            max_ref[p, b] = peak
            acc_ref[p, b] = product

    def back_start(p):
        for b in range(blocks):
            sums = acc_ref[p, b]
            result = sums[:, HD:] / sums[:, :HD]
            done_ref[p, :, pl.ds(b * size, size), :] = result.astype(BF16).reshape(zs, size, HD)
        for source in range(zs):
            att_send[p, source] = jnp.concatenate(
                [done_ref[p, source, pl.ds(0, quarter), :], done_ref[p, source, pl.ds(quarter, quarter), :]], axis=1
            )
        for source in range(zs):

            @pl.when(came(source))
            def _():
                att_recv[p, own_head] = att_send[p, source]

            @pl.when(jnp.logical_not(came(source)))
            def _():
                back_copy(p, source).start()

    def back_copy(p, source):
        return to_source(
            source, att_send.at[p, source], att_recv.at[p, own_head], att_ss.at[p, source], att_rs.at[p, own_head]
        )

    def back_wait(p):
        for h in range(heads):

            @pl.when(jnp.logical_not(stays(h)))
            def _():
                to_head(h, att_send.at[p, 0], att_recv.at[p, h], att_ss.at[p, 0], att_rs.at[p, h]).wait_recv()

    def columns(index):
        return pl.ds(pl.multiple_of(index * feats, feats), feats)

    pair_order = [2, 1, 3, 0] if nx == 4 else [1, 0] if nx == 2 else [0]
    pair_copies = [[None] * nx, [None] * nx]
    part_copies = [[], []]

    def pair_sums(p):
        joined = [att_recv[p, h] for h in range(heads)]
        attended = jnp.concatenate(
            [
                jnp.concatenate([packed[:, :HD] for packed in joined], axis=1),
                jnp.concatenate([packed[:, HD:] for packed in joined], axis=1),
            ],
            axis=0,
        )
        for dx in pair_order:
            other = lax.rem(x + dx, nx)
            pair_send[p, dx] = dot(attended, wo_ref[:, columns(other * 2 + 1 - core)]).astype(BF16)
            copy = remote(
                pair_send.at[p, dx], pair_recv.at[p, dx], pair_ss.at[p, dx], pair_rs.at[p, dx], tp=sibling
            )
            copy.start()
            pair_copies[p][dx] = copy
        for dx in pair_order:
            other = lax.rem(x + dx, nx)
            own_ref[p, dx] = dot(attended, wo_ref[:, columns(other * 2 + core)])

    def part_sums(p):
        for dx in pair_order[:-1]:
            other = lax.rem(x + dx, nx)
            pair_copies[p][dx].wait()
            part_send[p, dx] = (own_ref[p, dx] + pair_recv[p, dx].astype(F32)).astype(BF16)
            copy = remote(
                part_send.at[p, dx], part_recv.at[p, dx], part_ss.at[p, dx], part_rs.at[p, dx], tp=other * 2 + core
            )
            copy.start()
            part_copies[p].append(copy)

    def finish_rows(p):
        pair_copies[p][0].wait()
        projected = own_ref[p, 0] + pair_recv[p, 0].astype(F32)
        for copy in part_copies[p]:
            copy.wait()
        for dx in range(1, nx):
            projected = projected + part_recv[p, dx].astype(F32)
        gated_ref[pl.ds(p * half, half), :] = (gating[p] * projected).astype(BF16)

    near_by = [lax.rem(y + d, ny) for d in range(1, ny, 2)]
    far_off = [lax.rem(y + d, ny) for d in range(2, ny, 2)]

    def keys_in(p):
        deal_heads_wait(p, kv_send, kv_at, kvz_ss, kvz_rs)
        blocks_kv[p].start()

    def attend_own(p):
        blocks_kv[p].from_sibling(y)
        attend(p, [(y, core), (y, 1 - core)], True)

    def attend_near(p):
        if near_by:
            attend(p, [(pos, core) for pos in near_by])

    def attend_near_other(p):
        if near_by:
            for pos in near_by:
                blocks_kv[p].from_sibling(pos)
            attend(p, [(pos, 1 - core) for pos in near_by])

    def attend_far(p):
        for pos in far_off:
            blocks_kv[p].from_sibling(pos)
            attend(p, [(pos, core), (pos, 1 - core)])

    keys_in(0)
    queries_in(0)
    attend_own(0)
    keys_in(1)
    blocks_kv[0].near()
    attend_near(0)
    queries_in(1)
    attend_own(1)
    blocks_kv[0].far()
    attend_near_other(0)
    blocks_kv[1].near()
    attend_far(0)
    back_start(0)
    attend_near(1)
    blocks_kv[1].far()
    attend_near_other(1)
    back_wait(0)
    pair_sums(0)
    attend_far(1)
    back_start(1)
    part_sums(0)
    back_wait(1)
    pair_sums(1)
    part_sums(1)
    finish_rows(0)
    finish_rows(1)

    back_send[...] = dot(spread, gated_ref[...]).astype(BF16)
    exchange(back_send, back_recv, back_ss, back_rs)
    for p in (0, 1):
        features[p].finish()
        blocks_kv[p].finish()
        deal_heads_sent(p, kv_send, kv_at, kvz_ss, kvz_rs)
        deal_heads_sent(p, q_send, q_at, qz_ss, qz_rs)
        for source in range(zs):

            @pl.when(jnp.logical_not(came(source)))
            def _():
                back_copy(p, source).wait_send()

    exchange_wait(back_send, back_recv, back_ss, back_rs)
    out_ref[...] = dot(undeal, back_recv[...]).astype(BF16)


def build(cfg, tokens, router, gain, w_query, w_key, w_value, w_out, counts, picked):
    ny, nz, nx = cfg["ny"], cfg["nz"], cfg["nx"]
    rows, chunk, blocks = cfg["rows"], cfg["chunk"], cfg["blocks"]
    ctx, tp = ny * nz, nx * 2
    feats = tokens.shape[1]
    cap = picked.shape[1]
    slots = ctx * chunk
    half = rows // 2
    width = feats * tp
    heads = feats // HD
    zs = nz // 2
    tile = zs * (half // blocks)
    vmem = pl.BlockSpec(memory_space=pltpu.VMEM)
    hbm = pl.BlockSpec(memory_space=pltpu.HBM)
    dma = pltpu.SemaphoreType.DMA
    return pl.pallas_call(
        functools.partial(kernel, cfg),
        out_shape=jax.ShapeDtypeStruct((cap, feats), BF16),
        in_specs=[pl.BlockSpec(memory_space=pltpu.SMEM)] + [vmem] * 2 + [hbm] * 6,
        out_specs=vmem,
        scratch_shapes=[
            pltpu.VMEM(picked.shape, I32),
            pltpu.VMEM(tokens.shape, BF16),
            pltpu.VMEM((width, feats), BF16),
            pltpu.VMEM((width, feats), BF16),
            pltpu.VMEM((width, feats), BF16),
            pltpu.VMEM((feats, width), BF16),
            pltpu.VMEM((slots, feats), BF16),
            pltpu.VMEM((slots, feats), BF16),
            pltpu.VMEM((2, tp, half + 16, feats), BF16),
            pltpu.VMEM((2, half, width), BF16),
            pltpu.VMEM((2, heads, half, 2 * HD), BF16),
            pltpu.VMEM((ny, 2, 2, zs, half, 2 * HD), BF16),
            pltpu.VMEM((2, heads, half // 2, 2 * HD), BF16),
            pltpu.VMEM((2, zs, half // 2, 2 * HD), BF16),
            pltpu.VMEM((2, zs, half, 2 * HD), BF16),
            pltpu.VMEM((ny, 2, 2, zs, half, 2 * HD), BF16),
            pltpu.VMEM((2, blocks, tile, 1), F32),
            pltpu.VMEM((2, blocks, tile, 2 * HD), F32),
            pltpu.VMEM((2, zs, half, HD), BF16),
            pltpu.VMEM((rows, feats), BF16),
            pltpu.VMEM((2, zs, half // 2, 2 * HD), BF16),
            pltpu.VMEM((2, heads, half // 2, 2 * HD), BF16),
            pltpu.VMEM((2, nx, half, feats), BF16),
            pltpu.VMEM((2, nx, half, feats), BF16),
            pltpu.VMEM((2, nx, half, feats), F32),
            pltpu.VMEM((2, nx, half, feats), BF16),
            pltpu.VMEM((2, nx, half, feats), BF16),
            pltpu.VMEM((slots, feats), BF16),
            pltpu.VMEM((slots, feats), BF16),
            dma((6,)),
            dma((ctx,)),
            dma((ctx,)),
            dma((2, 2 * nx)),
            dma((2, nx, 2)),
            dma((2, heads)),
            dma((2, zs)),
            dma((2, heads)),
            dma((2, zs)),
            dma((2, 4 * ny + 4)),
            dma((2, ny, 2, 2)),
            dma((2, zs)),
            dma((2, heads)),
            dma((2, nx)),
            dma((2, nx)),
            dma((2, nx)),
            dma((2, nx)),
            dma((ctx,)),
            dma((ctx,)),
        ],
        compiler_params=pltpu.CompilerParams(
            collective_id=0, has_side_effects=True, vmem_limit_bytes=VMEM_BYTES
        ),
    )(counts, gain, router, picked, tokens, w_query, w_key, w_value, w_out)


def solution(mesh, nz=8, selected=6144, cap=384, blocks=1):
    ctx, tp = mesh.shape["ctx"], mesh.shape["tp"]
    per = -(-cap // ctx)
    cfg = {
        "ny": ctx // nz,
        "nz": nz,
        "nx": tp // 2,
        "rows": selected // ctx,
        "chunk": -(-per // 16) * 16,
        "blocks": blocks,
    }
    return jax.shard_map(
        functools.partial(build, cfg),
        mesh=mesh,
        in_specs=(
            P("ctx", "tp"),
            P("tp"),
            P("tp"),
            P(None, "tp"),
            P(None, "tp"),
            P(None, "tp"),
            P("tp", None),
            P(),
            P(),
        ),
        out_specs=P("ctx", "tp"),
        check_vma=False,
    )
```

```python
import functools
import math

import jax
import jax.numpy as jnp
from jax import lax
from jax.experimental import pallas as pl
from jax.experimental.pallas import tpu as pltpu
from jax.sharding import PartitionSpec as P

HD = 64
EPSILON = 1e-05
NEG_FILL = -1e30
MESH = pl.DeviceIdType.MESH
BF16 = jnp.bfloat16
F32 = jnp.float32
I32 = jnp.int32
VMEM_BYTES = 60 * 1024 * 1024


def iota(shape, dim):
    return lax.broadcasted_iota(I32, shape, dim)


def one_hot(mask):
    return jnp.where(mask, 1.0, 0.0).astype(BF16)


def dot(a, b):
    return jnp.dot(a, b, preferred_element_type=F32)


def dot_t(a, b):
    return lax.dot_general(a, b, (((1,), (1,)), ((), ())), preferred_element_type=F32)


def remote(src, dst, send, recv, **where):
    return pltpu.make_async_remote_copy(
        src_ref=src, dst_ref=dst, send_sem=send, recv_sem=recv, device_id=where, device_id_type=MESH
    )


class RingGather:
    def __init__(self, n, pos, core, view, ss, rs, device, sibling, parts=2):
        self.n, self.pos, self.core, self.view, self.ss, self.rs = n, pos, core, view, ss, rs
        self.device, self.sibling, self.parts = device, sibling, parts
        self.sent = []

    def at(self, step):
        return lax.rem(self.pos + step + self.n, self.n)

    def copy(self, pos, which, part, target):
        view = self.view(pos, which, part)
        return remote(view, view, self.ss(len(self.sent)), self.rs(pos, which, part), **target)

    def send(self, pos, part, target):
        copy = self.copy(pos, self.core, part, target)
        copy.start()
        self.sent.append(copy)

    def wait(self, pos, which, part):
        view = self.view(pos, which, part)
        remote(view, view, self.ss(0), self.rs(pos, which, part), **self.sibling).wait_recv()

    def start(self):
        right, left = self.device(self.at(1)), self.device(self.at(-1))
        parts = range(self.parts)
        for part in parts:
            if self.n > 1:
                self.send(self.pos, part, right)
            if self.n > 2:
                self.send(self.pos, self.parts - 1 - part, left)
        for part in parts:
            self.send(self.pos, part, self.sibling)

    def near(self):
        if self.n == 1:
            return
        right, left = self.device(self.at(1)), self.device(self.at(-1))
        for turn in range(self.parts):
            for step in (-1, 1) if self.n > 2 else (-1,):
                part = turn if step == -1 else self.parts - 1 - turn
                self.wait(self.at(step), self.core, part)
                if self.n > 2 and (turn == 0 and self.parts == 2 or self.parts == 1 and step == -1):
                    self.send(self.at(step), part, right if step == -1 else left)
                self.send(self.at(step), part, self.sibling)

    def far(self):
        if self.n > 2:
            for part in range(self.parts):
                self.wait(self.at(2), self.core, part)
                self.send(self.at(2), part, self.sibling)

    def from_sibling(self, pos):
        for part in range(self.parts):
            self.wait(pos, 1 - self.core, part)

    def finish(self):
        for copy in self.sent:
            copy.wait_send()


class Gather:
    def __init__(self, n, pos, core, view, ss, rs, device, sibling):
        self.n, self.pos, self.core, self.view, self.ss, self.rs = n, pos, core, view, ss, rs
        self.device, self.sibling = device, sibling
        self.sent = []

    def at(self, step):
        return lax.rem(self.pos + step, self.n)

    def copy(self, pos, which, slot, target):
        view = self.view(pos, which)
        return remote(view, view, self.ss(slot), self.rs(pos, which), **target)

    def send(self, pos, target):
        copy = self.copy(pos, self.core, len(self.sent), target)
        copy.start()
        self.sent.append(copy)

    def steps(self):
        return sorted(range(1, self.n), key=lambda d: min(d, self.n - d))

    def start(self):
        self.send(self.pos, self.sibling)
        for step in self.steps():
            self.send(self.pos, self.device(self.at(step)))

    def pass_on(self, step):
        self.copy(self.at(step), self.core, 0, self.sibling).wait_recv()
        self.send(self.at(step), self.sibling)

    def from_sibling(self, pos):
        self.copy(pos, 1 - self.core, 0, self.sibling).wait_recv()

    def finish(self):
        for copy in self.sent:
            copy.wait_send()


def kernel(
    cfg,
    counts_ref,
    gain_ref,
    router_ref,
    picked_hbm,
    tokens_hbm,
    wq_hbm,
    wk_hbm,
    wv_hbm,
    wo_hbm,
    out_ref,
    picked_ref,
    tokens_ref,
    wq_ref,
    wk_ref,
    wv_ref,
    wo_ref,
    row_send,
    row_recv,
    gathered,
    normed_ref,
    kv_send,
    kv_ref,
    q_send,
    q_recv,
    q_ref,
    value_ref,
    max_ref,
    acc_ref,
    done_ref,
    gated_ref,
    att_send,
    att_recv,
    pair_send,
    pair_recv,
    own_ref,
    part_send,
    part_recv,
    back_send,
    back_recv,
    w_sem,
    row_ss,
    row_rs,
    gat_ss,
    gat_rs,
    kvz_ss,
    kvz_rs,
    qz_ss,
    qz_rs,
    kvy_ss,
    kvy_rs,
    att_ss,
    att_rs,
    pair_ss,
    pair_rs,
    part_ss,
    part_rs,
    back_ss,
    back_rs,
):
    ny, nz, nx = cfg["ny"], cfg["nz"], cfg["nx"]
    rows, chunk, blocks = cfg["rows"], cfg["chunk"], cfg["blocks"]
    ctx, tp = ny * nz, nx * 2
    seq, feats = tokens_ref.shape
    cap = picked_ref.shape[1]
    slots = ctx * chunk
    shift = chunk.bit_length() - 1
    half = rows // 2
    quarter = half // 2
    width = feats * tp
    heads = feats // HD
    zs = nz // 2

    loads = [
        pltpu.make_async_copy(src, dst, w_sem.at[i])
        for i, (src, dst) in enumerate(
            (
                (picked_hbm, picked_ref),
                (tokens_hbm, tokens_ref),
                (wk_hbm, wk_ref),
                (wv_hbm, wv_ref),
                (wq_hbm, wq_ref),
                (wo_hbm, wo_ref),
            )
        )
    ]
    for copy in loads:
        copy.start()

    c = lax.axis_index("ctx")
    t = lax.axis_index("tp")
    y, z = c // nz, lax.rem(c, nz)
    x, core = t // 2, lax.rem(t, 2)
    sibling = x * 2 + 1 - core

    barrier = pltpu.get_barrier_semaphore()

    def greet(i, _):
        pl.semaphore_signal(
            barrier, inc=1, device_id={"ctx": lax.rem(c + i, ctx)}, device_id_type=MESH
        )
        return 0

    lax.fori_loop(1, ctx, greet, 0)
    for dx in range(1, nx):
        pl.semaphore_signal(
            barrier,
            inc=1,
            device_id={"tp": lax.rem(x + dx, nx) * 2 + core},
            device_id_type=MESH,
        )
    pl.semaphore_signal(barrier, inc=1, device_id={"tp": sibling}, device_id_type=MESH)
    for dz in range(1, nz):
        pl.semaphore_signal(
            barrier,
            inc=1,
            device_id={"ctx": y * nz + lax.rem(z + dz, nz), "tp": sibling},
            device_id_type=MESH,
        )

    own_count = counts_ref[c]
    own_offset = jnp.int32(0)
    for i in range(ctx):
        own_offset = own_offset + jnp.where(i < c, counts_ref[i], 0)
    loads[0].wait()
    place_row = picked_ref[pl.ds(c, 1), :] - c * seq
    place_col = jnp.broadcast_to(place_row, (8, cap)).T[:, :1]
    live_row = iota((1, cap), 1) < own_count
    live_col = iota((cap, 1), 0) < own_count
    before_row = jnp.where(live_col & (place_col < place_row), 1.0, 0.0)
    order_row = jnp.where(live_row, jnp.sum(before_row, axis=0, keepdims=True).astype(I32), -1)

    def wanted(index):
        dest, number = index >> shift, index & (chunk - 1)
        return ((dest - own_offset) & (ctx - 1)) + ctx * number

    deal = one_hot(wanted(iota((slots, 1), 0)) == order_row)
    pick = one_hot(place_col == iota((cap, seq), 1))
    loads[1].wait()
    picked_rows = dot(pick, tokens_ref[...]).astype(BF16)
    row_send[...] = dot(deal, picked_rows).astype(BF16)

    pl.semaphore_wait(barrier, ctx - 1 + nx + nz - 1)

    def span(i):
        return pl.ds(pl.multiple_of(i * chunk, chunk), chunk)

    def exchange(send_ref, recv_ref, ss, rs):
        def begin(i, _):
            d = lax.rem(c + i, ctx)
            remote(
                send_ref.at[span(d)], recv_ref.at[span(c)], ss.at[d], rs.at[c], ctx=d
            ).start()
            return 0

        lax.fori_loop(1, ctx, begin, 0)
        recv_ref[span(c), :] = send_ref[span(c), :]

    def exchange_wait(send_ref, recv_ref, ss, rs):
        def end(i, _):
            d = lax.rem(c + i, ctx)
            remote(send_ref.at[span(d)], recv_ref.at[span(d)], ss.at[d], rs.at[d], ctx=d).wait()
            return 0

        lax.fori_loop(1, ctx, end, 0)

    exchange(row_send, row_recv, row_ss, row_rs)

    source = iota((8, slots), 1) >> shift
    offset_of = jnp.zeros((8, slots), I32)
    count_of = jnp.zeros((8, slots), I32)
    for i in range(ctx):
        count = counts_ref[i]
        offset_of = offset_of + jnp.where(source > i, count, 0)
        count_of = count_of + jnp.where(source == i, count, 0)
    number = ((c - offset_of) & (ctx - 1)) + ctx * (iota((8, slots), 1) & (chunk - 1))
    local_index = jnp.where(number < count_of, (offset_of + number - c) >> (ctx.bit_length() - 1), -1)
    compact = one_hot(local_index[:1] == iota((rows, slots), 0))
    spread_index = local_index.T[:, :1]
    spread = one_hot(spread_index == iota((slots, rows), 1))

    before_col = jnp.where(live_row & (place_row < place_col), 1.0, 0.0)
    order_col = jnp.where(live_col, jnp.sum(before_col, axis=1, keepdims=True).astype(I32), -1)
    undeal = one_hot(order_col == wanted(iota((1, slots), 1)))

    exchange_wait(row_send, row_recv, row_ss, row_rs)

    packed_rows = dot(compact, row_recv[...]).astype(BF16)
    params = jnp.concatenate(
        [
            gain_ref[...].astype(F32).reshape(1, feats),
            router_ref[...].astype(F32).reshape(1, feats),
            jnp.zeros((14, feats), F32),
        ],
        axis=0,
    )
    gathered[0, t, pl.ds(0, half), :] = packed_rows[:half]
    gathered[0, t, pl.ds(half, 16), :] = params.astype(BF16)
    gathered[1, t, pl.ds(0, half), :] = packed_rows[half:]

    def feature_gather(p):
        height = half + 16 if p == 0 else half
        return Gather(
            nx,
            x,
            core,
            lambda pos, which: gathered.at[p, pos * 2 + which, pl.ds(0, height), :],
            lambda slot: gat_ss.at[p, slot],
            lambda pos, which: gat_rs.at[p, pos, which],
            lambda pos: {"tp": pos * 2 + core},
            {"tp": sibling},
        )

    features = [feature_gather(0), feature_gather(1)]
    features[0].start()
    features[1].start()

    zi, parity = z // 2, lax.rem(z, 2)
    head_core = z // heads
    own_head = lax.rem(z, heads)

    def stays(h):
        return (heads * core + h == z) & (parity == core)

    def came(source):
        return (source * 2 + core == z) & (head_core == core)

    def to_head(h, src, dst, ss, rs):
        return remote(src, dst, ss, rs, ctx=y * nz + heads * core + h, tp=x * 2 + parity)

    def to_source(source, src, dst, ss, rs):
        return remote(src, dst, ss, rs, ctx=y * nz + source * 2 + core, tp=x * 2 + head_core)

    def kv_at(p, source, which):
        return kv_ref.at[y, which, p, source]

    def q_at(p, source, which):
        return q_recv.at[p, source]

    def deal_heads(p, send_ref, target, ss, rs):
        for h in range(heads):

            @pl.when(stays(h))
            def _():
                target(p, zi, core)[...] = send_ref[p, h]

            @pl.when(jnp.logical_not(stays(h)))
            def _():
                to_head(h, send_ref.at[p, h], target(p, zi, parity), ss.at[p, h], rs.at[p, zi]).start()

    def deal_heads_wait(p, send_ref, target, ss, rs):
        for source in range(zs):

            @pl.when(jnp.logical_not(came(source)))
            def _():
                to_source(
                    source, send_ref.at[p, 0], target(p, source, core), ss.at[p, 0], rs.at[p, source]
                ).wait_recv()

    def deal_heads_sent(p, send_ref, target, ss, rs):
        for h in range(heads):

            @pl.when(jnp.logical_not(stays(h)))
            def _():
                to_head(h, send_ref.at[p, h], target(p, zi, parity), ss.at[p, h], rs.at[p, zi]).wait_send()

    def project(p):
        squares = jnp.zeros((half, feats), F32)
        routes = jnp.zeros((half, feats), F32)
        for b in range(tp):
            wide = gathered[p, b, pl.ds(0, half), :].astype(F32)
            params = gathered[0, b, pl.ds(half, 16), :].astype(F32)
            squares = squares + wide * wide
            routes = routes + wide * params[1:2]
        scale = lax.rsqrt(jnp.sum(squares, axis=1, keepdims=True) / width + EPSILON)
        for b in range(tp):
            wide = gathered[p, b, pl.ds(0, half), :].astype(F32)
            params = gathered[0, b, pl.ds(half, 16), :].astype(F32)
            normed_ref[p, :, pl.ds(b * feats, feats)] = (wide * scale * params[0:1]).astype(BF16)
        normed = normed_ref[p]
        keys = dot(normed, wk_ref[...]).astype(BF16)
        values = dot(normed, wv_ref[...]).astype(BF16)
        for h in range(heads):
            cols = slice(h * HD, (h + 1) * HD)
            kv_send[p, h] = jnp.concatenate([keys[:, cols], values[:, cols]], axis=1)
        deal_heads(p, kv_send, kv_at, kvz_ss, kvz_rs)
        queries = (dot(normed, wq_ref[...]).astype(BF16).astype(F32) * (1.0 / math.sqrt(HD))).astype(BF16)
        for h in range(heads):
            cols = slice(h * HD, (h + 1) * HD)
            q_send[p, h] = jnp.concatenate([queries[:quarter, cols], queries[quarter:, cols]], axis=1)
        deal_heads(p, q_send, q_at, qz_ss, qz_rs)
        return 1.0 / (1.0 + jnp.exp(-jnp.sum(routes, axis=1, keepdims=True)))

    def gather_end(p):
        for step in features[p].steps():
            features[p].pass_on(step)
        for pos in range(nx):
            features[p].from_sibling(pos)

    gather_end(0)
    for copy in loads[2:]:
        copy.wait()
    gating = [project(0)]
    gather_end(1)
    gating.append(project(1))

    kv_parts = 2 if zs > 1 else 1

    def kv_gather(p):
        split = (zs + 1) // 2
        return RingGather(
            ny,
            y,
            core,
            lambda pos, which, part: kv_ref.at[
                pos, which, p, pl.ds(0, split) if part == 0 else pl.ds(split, zs - split)
            ],
            lambda slot: kvy_ss.at[p, slot],
            lambda pos, which, part: kvy_rs.at[p, pos, which, part],
            lambda pos: {"ctx": pos * nz + z},
            {"tp": sibling},
            parts=kv_parts,
        )

    blocks_kv = [kv_gather(0), kv_gather(1)]
    size = half // blocks
    tile = zs * size
    tile_row = iota((tile, 1), 0)
    tile_col = iota((1, tile), 1)
    query_key = lax.rem(tile_row, size) * ctx + y * nz + (tile_row // size) * 2 + core
    key_base = lax.rem(tile_col, size) * ctx + (tile_col // size) * 2
    value_lane = iota((1, 1, 2 * HD), 2) >= HD
    zeros = jnp.zeros((quarter, HD), BF16)

    def queries_in(p):
        deal_heads_wait(p, q_send, q_at, qz_ss, qz_rs)
        for source in range(zs):
            packed = q_recv[p, source]
            q_ref[p, source, pl.ds(0, quarter), :] = jnp.concatenate([packed[:, :HD], zeros], axis=1)
            q_ref[p, source, pl.ds(quarter, quarter), :] = jnp.concatenate([packed[:, HD:], zeros], axis=1)

    def attend(p, pairs, first=False):
        allowed = []
        for pos, which in pairs:
            value_ref[pos, which, p] = jnp.where(value_lane, kv_ref[pos, which, p], jnp.ones((), BF16))
            allowed.append(key_base + (pos * nz + which) <= query_key)
        for b in range(blocks):
            now = pl.ds(b * size, size)
            q = q_ref[p, :, now, :].reshape(tile, 2 * HD)
            scores, operands = [], []
            for i, (pos, which) in enumerate(pairs):
                near = kv_ref[pos, which, p, :, now, :].reshape(tile, 2 * HD)
                scores.append(jnp.where(allowed[i], dot_t(q, near), NEG_FILL))
                operands.append(value_ref[pos, which, p, :, now, :].reshape(tile, 2 * HD))
                if b:
                    before = pl.ds(0, b * size)
                    past = kv_ref[pos, which, p, :, before, :].reshape(b * tile, 2 * HD)
                    scores.append(dot_t(q, past))
                    operands.append(value_ref[pos, which, p, :, before, :].reshape(b * tile, 2 * HD))
                if p:
                    scores.append(dot_t(q, kv_ref[pos, which, 0].reshape(zs * half, 2 * HD)))
                    operands.append(value_ref[pos, which, 0].reshape(zs * half, 2 * HD))
            peak = None if first else max_ref[p, b]
            for score in scores:
                top = jnp.max(score, axis=1, keepdims=True)
                peak = top if peak is None else jnp.maximum(peak, top)
            product = None if first else acc_ref[p, b] * jnp.exp(max_ref[p, b] - peak)
            for score, operand in zip(scores, operands):
                term = dot(jnp.exp(score - peak).astype(BF16), operand)
                product = term if product is None else product + term
            max_ref[p, b] = peak
            acc_ref[p, b] = product

    def back_start(p):
        for b in range(blocks):
            sums = acc_ref[p, b]
            result = sums[:, HD:] / sums[:, :HD]
            done_ref[p, :, pl.ds(b * size, size), :] = result.astype(BF16).reshape(zs, size, HD)
        for source in range(zs):
            att_send[p, source] = jnp.concatenate(
                [done_ref[p, source, pl.ds(0, quarter), :], done_ref[p, source, pl.ds(quarter, quarter), :]], axis=1
            )
        for source in range(zs):

            @pl.when(came(source))
            def _():
                att_recv[p, own_head] = att_send[p, source]

            @pl.when(jnp.logical_not(came(source)))
            def _():
                back_copy(p, source).start()

    def back_copy(p, source):
        return to_source(
            source, att_send.at[p, source], att_recv.at[p, own_head], att_ss.at[p, source], att_rs.at[p, own_head]
        )

    def back_wait(p):
        for h in range(heads):

            @pl.when(jnp.logical_not(stays(h)))
            def _():
                to_head(h, att_send.at[p, 0], att_recv.at[p, h], att_ss.at[p, 0], att_rs.at[p, h]).wait_recv()

    def columns(index):
        return pl.ds(pl.multiple_of(index * feats, feats), feats)

    pair_order = [2, 1, 3, 0] if nx == 4 else [1, 0] if nx == 2 else [0]
    pair_copies = [[None] * nx, [None] * nx]
    part_copies = [[], []]

    def pair_sums(p):
        joined = [att_recv[p, h] for h in range(heads)]
        attended = jnp.concatenate(
            [
                jnp.concatenate([packed[:, :HD] for packed in joined], axis=1),
                jnp.concatenate([packed[:, HD:] for packed in joined], axis=1),
            ],
            axis=0,
        )
        for dx in pair_order:
            other = lax.rem(x + dx, nx)
            pair_send[p, dx] = dot(attended, wo_ref[:, columns(other * 2 + 1 - core)]).astype(BF16)
            copy = remote(
                pair_send.at[p, dx], pair_recv.at[p, dx], pair_ss.at[p, dx], pair_rs.at[p, dx], tp=sibling
            )
            copy.start()
            pair_copies[p][dx] = copy
        for dx in pair_order:
            other = lax.rem(x + dx, nx)
            own_ref[p, dx] = dot(attended, wo_ref[:, columns(other * 2 + core)])

    def part_sums(p):
        for dx in pair_order[:-1]:
            other = lax.rem(x + dx, nx)
            pair_copies[p][dx].wait()
            part_send[p, dx] = (own_ref[p, dx] + pair_recv[p, dx].astype(F32)).astype(BF16)
            copy = remote(
                part_send.at[p, dx], part_recv.at[p, dx], part_ss.at[p, dx], part_rs.at[p, dx], tp=other * 2 + core
            )
            copy.start()
            part_copies[p].append(copy)

    def finish_rows(p):
        pair_copies[p][0].wait()
        projected = own_ref[p, 0] + pair_recv[p, 0].astype(F32)
        for copy in part_copies[p]:
            copy.wait()
        for dx in range(1, nx):
            projected = projected + part_recv[p, dx].astype(F32)
        gated_ref[pl.ds(p * half, half), :] = (gating[p] * projected).astype(BF16)

    near_by = [lax.rem(y + d, ny) for d in range(1, ny, 2)]
    far_off = [lax.rem(y + d, ny) for d in range(2, ny, 2)]

    def keys_in(p):
        deal_heads_wait(p, kv_send, kv_at, kvz_ss, kvz_rs)
        blocks_kv[p].start()

    def attend_own(p):
        blocks_kv[p].from_sibling(y)
        attend(p, [(y, core), (y, 1 - core)], True)

    def attend_near(p):
        if near_by:
            attend(p, [(pos, core) for pos in near_by])

    def attend_near_other(p):
        if near_by:
            for pos in near_by:
                blocks_kv[p].from_sibling(pos)
            attend(p, [(pos, 1 - core) for pos in near_by])

    def attend_far(p):
        for pos in far_off:
            blocks_kv[p].from_sibling(pos)
            attend(p, [(pos, core), (pos, 1 - core)])

    keys_in(0)
    queries_in(0)
    attend_own(0)
    keys_in(1)
    blocks_kv[0].near()
    attend_near(0)
    queries_in(1)
    attend_own(1)
    blocks_kv[0].far()
    attend_near_other(0)
    blocks_kv[1].near()
    attend_far(0)
    back_start(0)
    attend_near(1)
    blocks_kv[1].far()
    attend_near_other(1)
    attend_far(1)
    back_start(1)
    back_wait(0)
    pair_sums(0)
    part_sums(0)
    back_wait(1)
    pair_sums(1)
    part_sums(1)
    finish_rows(0)
    finish_rows(1)

    back_send[...] = dot(spread, gated_ref[...]).astype(BF16)
    exchange(back_send, back_recv, back_ss, back_rs)
    for p in (0, 1):
        features[p].finish()
        blocks_kv[p].finish()
        deal_heads_sent(p, kv_send, kv_at, kvz_ss, kvz_rs)
        deal_heads_sent(p, q_send, q_at, qz_ss, qz_rs)
        for source in range(zs):

            @pl.when(jnp.logical_not(came(source)))
            def _():
                back_copy(p, source).wait_send()

    exchange_wait(back_send, back_recv, back_ss, back_rs)
    out_ref[...] = dot(undeal, back_recv[...]).astype(BF16)


def build(cfg, tokens, router, gain, w_query, w_key, w_value, w_out, counts, picked):
    ny, nz, nx = cfg["ny"], cfg["nz"], cfg["nx"]
    rows, chunk, blocks = cfg["rows"], cfg["chunk"], cfg["blocks"]
    ctx, tp = ny * nz, nx * 2
    feats = tokens.shape[1]
    cap = picked.shape[1]
    slots = ctx * chunk
    half = rows // 2
    width = feats * tp
    heads = feats // HD
    zs = nz // 2
    tile = zs * (half // blocks)
    vmem = pl.BlockSpec(memory_space=pltpu.VMEM)
    hbm = pl.BlockSpec(memory_space=pltpu.HBM)
    dma = pltpu.SemaphoreType.DMA
    return pl.pallas_call(
        functools.partial(kernel, cfg),
        out_shape=jax.ShapeDtypeStruct((cap, feats), BF16),
        in_specs=[pl.BlockSpec(memory_space=pltpu.SMEM)] + [vmem] * 2 + [hbm] * 6,
        out_specs=vmem,
        scratch_shapes=[
            pltpu.VMEM(picked.shape, I32),
            pltpu.VMEM(tokens.shape, BF16),
            pltpu.VMEM((width, feats), BF16),
            pltpu.VMEM((width, feats), BF16),
            pltpu.VMEM((width, feats), BF16),
            pltpu.VMEM((feats, width), BF16),
            pltpu.VMEM((slots, feats), BF16),
            pltpu.VMEM((slots, feats), BF16),
            pltpu.VMEM((2, tp, half + 16, feats), BF16),
            pltpu.VMEM((2, half, width), BF16),
            pltpu.VMEM((2, heads, half, 2 * HD), BF16),
            pltpu.VMEM((ny, 2, 2, zs, half, 2 * HD), BF16),
            pltpu.VMEM((2, heads, half // 2, 2 * HD), BF16),
            pltpu.VMEM((2, zs, half // 2, 2 * HD), BF16),
            pltpu.VMEM((2, zs, half, 2 * HD), BF16),
            pltpu.VMEM((ny, 2, 2, zs, half, 2 * HD), BF16),
            pltpu.VMEM((2, blocks, tile, 1), F32),
            pltpu.VMEM((2, blocks, tile, 2 * HD), F32),
            pltpu.VMEM((2, zs, half, HD), BF16),
            pltpu.VMEM((rows, feats), BF16),
            pltpu.VMEM((2, zs, half // 2, 2 * HD), BF16),
            pltpu.VMEM((2, heads, half // 2, 2 * HD), BF16),
            pltpu.VMEM((2, nx, half, feats), BF16),
            pltpu.VMEM((2, nx, half, feats), BF16),
            pltpu.VMEM((2, nx, half, feats), F32),
            pltpu.VMEM((2, nx, half, feats), BF16),
            pltpu.VMEM((2, nx, half, feats), BF16),
            pltpu.VMEM((slots, feats), BF16),
            pltpu.VMEM((slots, feats), BF16),
            dma((6,)),
            dma((ctx,)),
            dma((ctx,)),
            dma((2, 2 * nx)),
            dma((2, nx, 2)),
            dma((2, heads)),
            dma((2, zs)),
            dma((2, heads)),
            dma((2, zs)),
            dma((2, 4 * ny + 4)),
            dma((2, ny, 2, 2)),
            dma((2, zs)),
            dma((2, heads)),
            dma((2, nx)),
            dma((2, nx)),
            dma((2, nx)),
            dma((2, nx)),
            dma((ctx,)),
            dma((ctx,)),
        ],
        compiler_params=pltpu.CompilerParams(
            collective_id=0, has_side_effects=True, vmem_limit_bytes=VMEM_BYTES
        ),
    )(counts, gain, router, picked, tokens, w_query, w_key, w_value, w_out)


def solution(mesh, nz=8, selected=6144, cap=384, blocks=1):
    ctx, tp = mesh.shape["ctx"], mesh.shape["tp"]
    per = -(-cap // ctx)
    cfg = {
        "ny": ctx // nz,
        "nz": nz,
        "nx": tp // 2,
        "rows": selected // ctx,
        "chunk": -(-per // 16) * 16,
        "blocks": blocks,
    }
    return jax.shard_map(
        functools.partial(build, cfg),
        mesh=mesh,
        in_specs=(
            P("ctx", "tp"),
            P("tp"),
            P("tp"),
            P(None, "tp"),
            P(None, "tp"),
            P(None, "tp"),
            P("tp", None),
            P(),
            P(),
        ),
        out_specs=P("ctx", "tp"),
        check_vma=False,
    )
```

```python
import functools
import math

import jax
import jax.numpy as jnp
from jax import lax
from jax.experimental import pallas as pl
from jax.experimental.pallas import tpu as pltpu
from jax.sharding import PartitionSpec as P

HD = 64
EPSILON = 1e-05
NEG_FILL = -1e30
MESH = pl.DeviceIdType.MESH
BF16 = jnp.bfloat16
F32 = jnp.float32
I32 = jnp.int32
VMEM_BYTES = 60 * 1024 * 1024


def iota(shape, dim):
    return lax.broadcasted_iota(I32, shape, dim)


def one_hot(mask):
    return jnp.where(mask, 1.0, 0.0).astype(BF16)


def dot(a, b):
    return jnp.dot(a, b, preferred_element_type=F32)


def dot_t(a, b):
    return lax.dot_general(a, b, (((1,), (1,)), ((), ())), preferred_element_type=F32)


def remote(src, dst, send, recv, **where):
    return pltpu.make_async_remote_copy(
        src_ref=src, dst_ref=dst, send_sem=send, recv_sem=recv, device_id=where, device_id_type=MESH
    )


class RingGather:
    def __init__(self, n, pos, core, view, ss, rs, device, sibling, parts=2):
        self.n, self.pos, self.core, self.view, self.ss, self.rs = n, pos, core, view, ss, rs
        self.device, self.sibling, self.parts = device, sibling, parts
        self.sent = []

    def at(self, step):
        return lax.rem(self.pos + step + self.n, self.n)

    def copy(self, pos, which, part, target):
        view = self.view(pos, which, part)
        return remote(view, view, self.ss(len(self.sent)), self.rs(pos, which, part), **target)

    def send(self, pos, part, target):
        copy = self.copy(pos, self.core, part, target)
        copy.start()
        self.sent.append(copy)

    def wait(self, pos, which, part):
        view = self.view(pos, which, part)
        remote(view, view, self.ss(0), self.rs(pos, which, part), **self.sibling).wait_recv()

    def start(self):
        right, left = self.device(self.at(1)), self.device(self.at(-1))
        parts = range(self.parts)
        for part in parts:
            if self.n > 1:
                self.send(self.pos, part, right)
            if self.n > 2:
                self.send(self.pos, self.parts - 1 - part, left)
        for part in parts:
            self.send(self.pos, part, self.sibling)

    def near(self):
        if self.n == 1:
            return
        right, left = self.device(self.at(1)), self.device(self.at(-1))
        for turn in range(self.parts):
            for step in (-1, 1) if self.n > 2 else (-1,):
                part = turn if step == -1 else self.parts - 1 - turn
                self.wait(self.at(step), self.core, part)
                if self.n > 2 and (turn == 0 and self.parts == 2 or self.parts == 1 and step == -1):
                    self.send(self.at(step), part, right if step == -1 else left)
                self.send(self.at(step), part, self.sibling)

    def far(self):
        if self.n > 2:
            for part in range(self.parts):
                self.wait(self.at(2), self.core, part)
                self.send(self.at(2), part, self.sibling)

    def from_sibling(self, pos):
        for part in range(self.parts):
            self.wait(pos, 1 - self.core, part)

    def finish(self):
        for copy in self.sent:
            copy.wait_send()


class Gather:
    def __init__(self, n, pos, core, view, ss, rs, device, sibling):
        self.n, self.pos, self.core, self.view, self.ss, self.rs = n, pos, core, view, ss, rs
        self.device, self.sibling = device, sibling
        self.sent = []

    def at(self, step):
        return lax.rem(self.pos + step, self.n)

    def copy(self, pos, which, slot, target):
        view = self.view(pos, which)
        return remote(view, view, self.ss(slot), self.rs(pos, which), **target)

    def send(self, pos, target):
        copy = self.copy(pos, self.core, len(self.sent), target)
        copy.start()
        self.sent.append(copy)

    def steps(self):
        return sorted(range(1, self.n), key=lambda d: min(d, self.n - d))

    def start(self):
        self.send(self.pos, self.sibling)
        for step in self.steps():
            self.send(self.pos, self.device(self.at(step)))

    def pass_on(self, step):
        self.copy(self.at(step), self.core, 0, self.sibling).wait_recv()
        self.send(self.at(step), self.sibling)

    def from_sibling(self, pos):
        self.copy(pos, 1 - self.core, 0, self.sibling).wait_recv()

    def finish(self):
        for copy in self.sent:
            copy.wait_send()


def kernel(
    cfg,
    counts_ref,
    gain_ref,
    router_ref,
    picked_hbm,
    tokens_hbm,
    wq_hbm,
    wk_hbm,
    wv_hbm,
    wo_hbm,
    out_ref,
    picked_ref,
    tokens_ref,
    wq_ref,
    wk_ref,
    wv_ref,
    wo_ref,
    row_send,
    row_recv,
    gathered,
    normed_ref,
    kv_send,
    kv_ref,
    q_send,
    q_recv,
    q_ref,
    value_ref,
    max_ref,
    acc_ref,
    done_ref,
    gated_ref,
    att_send,
    att_recv,
    pair_send,
    pair_recv,
    own_ref,
    part_send,
    part_recv,
    back_send,
    back_recv,
    w_sem,
    row_ss,
    row_rs,
    gat_ss,
    gat_rs,
    kvz_ss,
    kvz_rs,
    qz_ss,
    qz_rs,
    kvy_ss,
    kvy_rs,
    att_ss,
    att_rs,
    pair_ss,
    pair_rs,
    part_ss,
    part_rs,
    back_ss,
    back_rs,
):
    ny, nz, nx = cfg["ny"], cfg["nz"], cfg["nx"]
    rows, chunk, blocks = cfg["rows"], cfg["chunk"], cfg["blocks"]
    ctx, tp = ny * nz, nx * 2
    seq, feats = tokens_ref.shape
    cap = picked_ref.shape[1]
    slots = ctx * chunk
    shift = chunk.bit_length() - 1
    half = rows // 2
    quarter = half // 2
    width = feats * tp
    heads = feats // HD
    zs = nz // 2

    loads = [
        pltpu.make_async_copy(src, dst, w_sem.at[i])
        for i, (src, dst) in enumerate(
            (
                (picked_hbm, picked_ref),
                (tokens_hbm, tokens_ref),
                (wk_hbm, wk_ref),
                (wv_hbm, wv_ref),
                (wq_hbm, wq_ref),
                (wo_hbm, wo_ref),
            )
        )
    ]
    for copy in loads:
        copy.start()

    c = lax.axis_index("ctx")
    t = lax.axis_index("tp")
    y, z = c // nz, lax.rem(c, nz)
    x, core = t // 2, lax.rem(t, 2)
    sibling = x * 2 + 1 - core

    barrier = pltpu.get_barrier_semaphore()

    def greet(i, _):
        pl.semaphore_signal(
            barrier, inc=1, device_id={"ctx": lax.rem(c + i, ctx)}, device_id_type=MESH
        )
        return 0

    lax.fori_loop(1, ctx, greet, 0)
    for dx in range(1, nx):
        pl.semaphore_signal(
            barrier,
            inc=1,
            device_id={"tp": lax.rem(x + dx, nx) * 2 + core},
            device_id_type=MESH,
        )
    pl.semaphore_signal(barrier, inc=1, device_id={"tp": sibling}, device_id_type=MESH)
    for dz in range(1, nz):
        pl.semaphore_signal(
            barrier,
            inc=1,
            device_id={"ctx": y * nz + lax.rem(z + dz, nz), "tp": sibling},
            device_id_type=MESH,
        )

    own_count = counts_ref[c]
    own_offset = jnp.int32(0)
    for i in range(ctx):
        own_offset = own_offset + jnp.where(i < c, counts_ref[i], 0)
    loads[0].wait()
    place_row = picked_ref[pl.ds(c, 1), :] - c * seq
    place_col = jnp.broadcast_to(place_row, (8, cap)).T[:, :1]
    live_row = iota((1, cap), 1) < own_count
    live_col = iota((cap, 1), 0) < own_count
    before_row = jnp.where(live_col & (place_col < place_row), 1.0, 0.0)
    order_row = jnp.where(live_row, jnp.sum(before_row, axis=0, keepdims=True).astype(I32), -1)

    def wanted(index):
        dest, number = index >> shift, index & (chunk - 1)
        return ((dest - own_offset) & (ctx - 1)) + ctx * number

    deal = one_hot(wanted(iota((slots, 1), 0)) == order_row)
    pick = one_hot(place_col == iota((cap, seq), 1))
    loads[1].wait()
    picked_rows = dot(pick, tokens_ref[...]).astype(BF16)
    row_send[...] = dot(deal, picked_rows).astype(BF16)

    pl.semaphore_wait(barrier, ctx - 1 + nx + nz - 1)

    def span(i):
        return pl.ds(pl.multiple_of(i * chunk, chunk), chunk)

    def exchange(send_ref, recv_ref, ss, rs):
        def begin(i, _):
            d = lax.rem(c + i, ctx)
            remote(
                send_ref.at[span(d)], recv_ref.at[span(c)], ss.at[d], rs.at[c], ctx=d
            ).start()
            return 0

        lax.fori_loop(1, ctx, begin, 0)
        recv_ref[span(c), :] = send_ref[span(c), :]

    def exchange_wait(send_ref, recv_ref, ss, rs):
        def end(i, _):
            d = lax.rem(c + i, ctx)
            remote(send_ref.at[span(d)], recv_ref.at[span(d)], ss.at[d], rs.at[d], ctx=d).wait()
            return 0

        lax.fori_loop(1, ctx, end, 0)

    exchange(row_send, row_recv, row_ss, row_rs)

    source = iota((8, slots), 1) >> shift
    offset_of = jnp.zeros((8, slots), I32)
    count_of = jnp.zeros((8, slots), I32)
    for i in range(ctx):
        count = counts_ref[i]
        offset_of = offset_of + jnp.where(source > i, count, 0)
        count_of = count_of + jnp.where(source == i, count, 0)
    number = ((c - offset_of) & (ctx - 1)) + ctx * (iota((8, slots), 1) & (chunk - 1))
    local_index = jnp.where(number < count_of, (offset_of + number - c) >> (ctx.bit_length() - 1), -1)
    compact = one_hot(local_index[:1] == iota((rows, slots), 0))
    spread_index = local_index.T[:, :1]
    spread = one_hot(spread_index == iota((slots, rows), 1))

    before_col = jnp.where(live_row & (place_row < place_col), 1.0, 0.0)
    order_col = jnp.where(live_col, jnp.sum(before_col, axis=1, keepdims=True).astype(I32), -1)
    undeal = one_hot(order_col == wanted(iota((1, slots), 1)))

    exchange_wait(row_send, row_recv, row_ss, row_rs)

    packed_rows = dot(compact, row_recv[...]).astype(BF16)
    params = jnp.concatenate(
        [
            gain_ref[...].astype(F32).reshape(1, feats),
            router_ref[...].astype(F32).reshape(1, feats),
            jnp.zeros((14, feats), F32),
        ],
        axis=0,
    )
    gathered[0, t, pl.ds(0, half), :] = packed_rows[:half]
    gathered[0, t, pl.ds(half, 16), :] = params.astype(BF16)
    gathered[1, t, pl.ds(0, half), :] = packed_rows[half:]

    def feature_gather(p):
        height = half + 16 if p == 0 else half
        return Gather(
            nx,
            x,
            core,
            lambda pos, which: gathered.at[p, pos * 2 + which, pl.ds(0, height), :],
            lambda slot: gat_ss.at[p, slot],
            lambda pos, which: gat_rs.at[p, pos, which],
            lambda pos: {"tp": pos * 2 + core},
            {"tp": sibling},
        )

    features = [feature_gather(0), feature_gather(1)]
    features[0].start()
    features[1].start()

    zi, parity = z // 2, lax.rem(z, 2)
    head_core = z // heads
    own_head = lax.rem(z, heads)

    def stays(h):
        return (heads * core + h == z) & (parity == core)

    def came(source):
        return (source * 2 + core == z) & (head_core == core)

    def to_head(h, src, dst, ss, rs):
        return remote(src, dst, ss, rs, ctx=y * nz + heads * core + h, tp=x * 2 + parity)

    def to_source(source, src, dst, ss, rs):
        return remote(src, dst, ss, rs, ctx=y * nz + source * 2 + core, tp=x * 2 + head_core)

    def kv_at(p, source, which):
        return kv_ref.at[y, which, p, source]

    def q_at(p, source, which):
        return q_recv.at[p, source]

    def deal_heads(p, send_ref, target, ss, rs):
        for h in range(heads):

            @pl.when(stays(h))
            def _():
                target(p, zi, core)[...] = send_ref[p, h]

            @pl.when(jnp.logical_not(stays(h)))
            def _():
                to_head(h, send_ref.at[p, h], target(p, zi, parity), ss.at[p, h], rs.at[p, zi]).start()

    def deal_heads_wait(p, send_ref, target, ss, rs):
        for source in range(zs):

            @pl.when(jnp.logical_not(came(source)))
            def _():
                to_source(
                    source, send_ref.at[p, 0], target(p, source, core), ss.at[p, 0], rs.at[p, source]
                ).wait_recv()

    def deal_heads_sent(p, send_ref, target, ss, rs):
        for h in range(heads):

            @pl.when(jnp.logical_not(stays(h)))
            def _():
                to_head(h, send_ref.at[p, h], target(p, zi, parity), ss.at[p, h], rs.at[p, zi]).wait_send()

    def project(p):
        squares = jnp.zeros((half, feats), F32)
        routes = jnp.zeros((half, feats), F32)
        for b in range(tp):
            wide = gathered[p, b, pl.ds(0, half), :].astype(F32)
            params = gathered[0, b, pl.ds(half, 16), :].astype(F32)
            squares = squares + wide * wide
            routes = routes + wide * params[1:2]
        scale = lax.rsqrt(jnp.sum(squares, axis=1, keepdims=True) / width + EPSILON)
        for b in range(tp):
            wide = gathered[p, b, pl.ds(0, half), :].astype(F32)
            params = gathered[0, b, pl.ds(half, 16), :].astype(F32)
            normed_ref[p, :, pl.ds(b * feats, feats)] = (wide * scale * params[0:1]).astype(BF16)
        normed = normed_ref[p]
        keys = dot(normed, wk_ref[...]).astype(BF16)
        values = dot(normed, wv_ref[...]).astype(BF16)
        for h in range(heads):
            cols = slice(h * HD, (h + 1) * HD)
            kv_send[p, h] = jnp.concatenate([keys[:, cols], values[:, cols]], axis=1)
        deal_heads(p, kv_send, kv_at, kvz_ss, kvz_rs)
        queries = (dot(normed, wq_ref[...]).astype(BF16).astype(F32) * (1.0 / math.sqrt(HD))).astype(BF16)
        for h in range(heads):
            cols = slice(h * HD, (h + 1) * HD)
            q_send[p, h] = jnp.concatenate([queries[:quarter, cols], queries[quarter:, cols]], axis=1)
        deal_heads(p, q_send, q_at, qz_ss, qz_rs)
        return 1.0 / (1.0 + jnp.exp(-jnp.sum(routes, axis=1, keepdims=True)))

    def gather_end(p):
        for step in features[p].steps():
            features[p].pass_on(step)
        for pos in range(nx):
            features[p].from_sibling(pos)

    gather_end(0)
    for copy in loads[2:]:
        copy.wait()
    gating = [project(0)]
    gather_end(1)
    gating.append(project(1))

    kv_parts = 2 if zs > 1 else 1

    def kv_gather(p):
        split = (zs + 1) // 2
        return RingGather(
            ny,
            y,
            core,
            lambda pos, which, part: kv_ref.at[
                pos, which, p, pl.ds(0, split) if part == 0 else pl.ds(split, zs - split)
            ],
            lambda slot: kvy_ss.at[p, slot],
            lambda pos, which, part: kvy_rs.at[p, pos, which, part],
            lambda pos: {"ctx": pos * nz + z},
            {"tp": sibling},
            parts=kv_parts,
        )

    blocks_kv = [kv_gather(0), kv_gather(1)]
    size = half // blocks
    tile = zs * size
    tile_row = iota((tile, 1), 0)
    tile_col = iota((1, tile), 1)
    query_key = lax.rem(tile_row, size) * ctx + y * nz + (tile_row // size) * 2 + core
    key_base = lax.rem(tile_col, size) * ctx + (tile_col // size) * 2
    value_lane = iota((1, 1, 2 * HD), 2) >= HD
    zeros = jnp.zeros((quarter, HD), BF16)

    def queries_in(p):
        deal_heads_wait(p, q_send, q_at, qz_ss, qz_rs)
        for source in range(zs):
            packed = q_recv[p, source]
            q_ref[p, source, pl.ds(0, quarter), :] = jnp.concatenate([packed[:, :HD], zeros], axis=1)
            q_ref[p, source, pl.ds(quarter, quarter), :] = jnp.concatenate([packed[:, HD:], zeros], axis=1)

    def attend(p, pairs, first=False):
        allowed = []
        for pos, which in pairs:
            value_ref[pos, which, p] = jnp.where(value_lane, kv_ref[pos, which, p], jnp.ones((), BF16))
            allowed.append(key_base + (pos * nz + which) <= query_key)
        for b in range(blocks):
            now = pl.ds(b * size, size)
            q = q_ref[p, :, now, :].reshape(tile, 2 * HD)
            scores, operands = [], []
            for i, (pos, which) in enumerate(pairs):
                near = kv_ref[pos, which, p, :, now, :].reshape(tile, 2 * HD)
                scores.append(jnp.where(allowed[i], dot_t(q, near), NEG_FILL))
                operands.append(value_ref[pos, which, p, :, now, :].reshape(tile, 2 * HD))
                if b:
                    before = pl.ds(0, b * size)
                    past = kv_ref[pos, which, p, :, before, :].reshape(b * tile, 2 * HD)
                    scores.append(dot_t(q, past))
                    operands.append(value_ref[pos, which, p, :, before, :].reshape(b * tile, 2 * HD))
                if p:
                    scores.append(dot_t(q, kv_ref[pos, which, 0].reshape(zs * half, 2 * HD)))
                    operands.append(value_ref[pos, which, 0].reshape(zs * half, 2 * HD))
            peak = None if first else max_ref[p, b]
            for score in scores:
                top = jnp.max(score, axis=1, keepdims=True)
                peak = top if peak is None else jnp.maximum(peak, top)
            product = None if first else acc_ref[p, b] * jnp.exp(max_ref[p, b] - peak)
            for score, operand in zip(scores, operands):
                term = dot(jnp.exp(score - peak).astype(BF16), operand)
                product = term if product is None else product + term
            max_ref[p, b] = peak
            acc_ref[p, b] = product

    def back_start(p):
        for b in range(blocks):
            sums = acc_ref[p, b]
            result = sums[:, HD:] / sums[:, :HD]
            done_ref[p, :, pl.ds(b * size, size), :] = result.astype(BF16).reshape(zs, size, HD)
        for source in range(zs):
            att_send[p, source] = jnp.concatenate(
                [done_ref[p, source, pl.ds(0, quarter), :], done_ref[p, source, pl.ds(quarter, quarter), :]], axis=1
            )
        for source in range(zs):

            @pl.when(came(source))
            def _():
                att_recv[p, own_head] = att_send[p, source]

            @pl.when(jnp.logical_not(came(source)))
            def _():
                back_copy(p, source).start()

    def back_copy(p, source):
        return to_source(
            source, att_send.at[p, source], att_recv.at[p, own_head], att_ss.at[p, source], att_rs.at[p, own_head]
        )

    def back_wait(p):
        for h in range(heads):

            @pl.when(jnp.logical_not(stays(h)))
            def _():
                to_head(h, att_send.at[p, 0], att_recv.at[p, h], att_ss.at[p, 0], att_rs.at[p, h]).wait_recv()

    def columns(index):
        return pl.ds(pl.multiple_of(index * feats, feats), feats)

    pair_order = [2, 1, 3, 0] if nx == 4 else [1, 0] if nx == 2 else [0]
    pair_copies = [[None] * nx, [None] * nx]
    part_copies = [[], []]

    def pair_sums(p):
        joined = [att_recv[p, h] for h in range(heads)]
        attended = jnp.concatenate(
            [
                jnp.concatenate([packed[:, :HD] for packed in joined], axis=1),
                jnp.concatenate([packed[:, HD:] for packed in joined], axis=1),
            ],
            axis=0,
        )
        for dx in pair_order:
            other = lax.rem(x + dx, nx)
            pair_send[p, dx] = dot(attended, wo_ref[:, columns(other * 2 + 1 - core)]).astype(BF16)
            copy = remote(
                pair_send.at[p, dx], pair_recv.at[p, dx], pair_ss.at[p, dx], pair_rs.at[p, dx], tp=sibling
            )
            copy.start()
            pair_copies[p][dx] = copy
        for dx in pair_order:
            other = lax.rem(x + dx, nx)
            own_ref[p, dx] = dot(attended, wo_ref[:, columns(other * 2 + core)])

    def part_sums(p):
        for dx in pair_order[:-1]:
            other = lax.rem(x + dx, nx)
            pair_copies[p][dx].wait()
            part_send[p, dx] = (own_ref[p, dx] + pair_recv[p, dx].astype(F32)).astype(BF16)
            copy = remote(
                part_send.at[p, dx], part_recv.at[p, dx], part_ss.at[p, dx], part_rs.at[p, dx], tp=other * 2 + core
            )
            copy.start()
            part_copies[p].append(copy)

    def finish_rows(p):
        pair_copies[p][0].wait()
        projected = own_ref[p, 0] + pair_recv[p, 0].astype(F32)
        for copy in part_copies[p]:
            copy.wait()
        for dx in range(1, nx):
            projected = projected + part_recv[p, dx].astype(F32)
        gated_ref[pl.ds(p * half, half), :] = (gating[p] * projected).astype(BF16)

    near_by = [lax.rem(y + d, ny) for d in range(1, ny, 2)]
    far_off = [lax.rem(y + d, ny) for d in range(2, ny, 2)]

    def keys_in(p):
        deal_heads_wait(p, kv_send, kv_at, kvz_ss, kvz_rs)
        blocks_kv[p].start()

    def attend_own(p):
        blocks_kv[p].from_sibling(y)
        attend(p, [(y, core), (y, 1 - core)], True)

    def attend_near(p):
        if near_by:
            attend(p, [(pos, core) for pos in near_by])

    def attend_near_other(p):
        if near_by:
            for pos in near_by:
                blocks_kv[p].from_sibling(pos)
            attend(p, [(pos, 1 - core) for pos in near_by])

    def attend_far(p):
        for pos in far_off:
            blocks_kv[p].from_sibling(pos)
            attend(p, [(pos, core), (pos, 1 - core)])

    keys_in(0)
    queries_in(0)
    attend_own(0)
    keys_in(1)
    blocks_kv[0].near()
    queries_in(1)
    attend_near(0)
    attend_own(1)
    blocks_kv[0].far()
    blocks_kv[1].near()
    attend_near_other(0)
    attend_far(0)
    back_start(0)
    attend_near(1)
    blocks_kv[1].far()
    attend_near_other(1)
    attend_far(1)
    back_start(1)
    back_wait(0)
    pair_sums(0)
    part_sums(0)
    back_wait(1)
    pair_sums(1)
    part_sums(1)
    finish_rows(0)
    finish_rows(1)

    back_send[...] = dot(spread, gated_ref[...]).astype(BF16)
    exchange(back_send, back_recv, back_ss, back_rs)
    for p in (0, 1):
        features[p].finish()
        blocks_kv[p].finish()
        deal_heads_sent(p, kv_send, kv_at, kvz_ss, kvz_rs)
        deal_heads_sent(p, q_send, q_at, qz_ss, qz_rs)
        for source in range(zs):

            @pl.when(jnp.logical_not(came(source)))
            def _():
                back_copy(p, source).wait_send()

    exchange_wait(back_send, back_recv, back_ss, back_rs)
    out_ref[...] = dot(undeal, back_recv[...]).astype(BF16)


def build(cfg, tokens, router, gain, w_query, w_key, w_value, w_out, counts, picked):
    ny, nz, nx = cfg["ny"], cfg["nz"], cfg["nx"]
    rows, chunk, blocks = cfg["rows"], cfg["chunk"], cfg["blocks"]
    ctx, tp = ny * nz, nx * 2
    feats = tokens.shape[1]
    cap = picked.shape[1]
    slots = ctx * chunk
    half = rows // 2
    width = feats * tp
    heads = feats // HD
    zs = nz // 2
    tile = zs * (half // blocks)
    vmem = pl.BlockSpec(memory_space=pltpu.VMEM)
    hbm = pl.BlockSpec(memory_space=pltpu.HBM)
    dma = pltpu.SemaphoreType.DMA
    return pl.pallas_call(
        functools.partial(kernel, cfg),
        out_shape=jax.ShapeDtypeStruct((cap, feats), BF16),
        in_specs=[pl.BlockSpec(memory_space=pltpu.SMEM)] + [vmem] * 2 + [hbm] * 6,
        out_specs=vmem,
        scratch_shapes=[
            pltpu.VMEM(picked.shape, I32),
            pltpu.VMEM(tokens.shape, BF16),
            pltpu.VMEM((width, feats), BF16),
            pltpu.VMEM((width, feats), BF16),
            pltpu.VMEM((width, feats), BF16),
            pltpu.VMEM((feats, width), BF16),
            pltpu.VMEM((slots, feats), BF16),
            pltpu.VMEM((slots, feats), BF16),
            pltpu.VMEM((2, tp, half + 16, feats), BF16),
            pltpu.VMEM((2, half, width), BF16),
            pltpu.VMEM((2, heads, half, 2 * HD), BF16),
            pltpu.VMEM((ny, 2, 2, zs, half, 2 * HD), BF16),
            pltpu.VMEM((2, heads, half // 2, 2 * HD), BF16),
            pltpu.VMEM((2, zs, half // 2, 2 * HD), BF16),
            pltpu.VMEM((2, zs, half, 2 * HD), BF16),
            pltpu.VMEM((ny, 2, 2, zs, half, 2 * HD), BF16),
            pltpu.VMEM((2, blocks, tile, 1), F32),
            pltpu.VMEM((2, blocks, tile, 2 * HD), F32),
            pltpu.VMEM((2, zs, half, HD), BF16),
            pltpu.VMEM((rows, feats), BF16),
            pltpu.VMEM((2, zs, half // 2, 2 * HD), BF16),
            pltpu.VMEM((2, heads, half // 2, 2 * HD), BF16),
            pltpu.VMEM((2, nx, half, feats), BF16),
            pltpu.VMEM((2, nx, half, feats), BF16),
            pltpu.VMEM((2, nx, half, feats), F32),
            pltpu.VMEM((2, nx, half, feats), BF16),
            pltpu.VMEM((2, nx, half, feats), BF16),
            pltpu.VMEM((slots, feats), BF16),
            pltpu.VMEM((slots, feats), BF16),
            dma((6,)),
            dma((ctx,)),
            dma((ctx,)),
            dma((2, 2 * nx)),
            dma((2, nx, 2)),
            dma((2, heads)),
            dma((2, zs)),
            dma((2, heads)),
            dma((2, zs)),
            dma((2, 4 * ny + 4)),
            dma((2, ny, 2, 2)),
            dma((2, zs)),
            dma((2, heads)),
            dma((2, nx)),
            dma((2, nx)),
            dma((2, nx)),
            dma((2, nx)),
            dma((ctx,)),
            dma((ctx,)),
        ],
        compiler_params=pltpu.CompilerParams(
            collective_id=0, has_side_effects=True, vmem_limit_bytes=VMEM_BYTES
        ),
    )(counts, gain, router, picked, tokens, w_query, w_key, w_value, w_out)


def solution(mesh, nz=8, selected=6144, cap=384, blocks=1):
    ctx, tp = mesh.shape["ctx"], mesh.shape["tp"]
    per = -(-cap // ctx)
    cfg = {
        "ny": ctx // nz,
        "nz": nz,
        "nx": tp // 2,
        "rows": selected // ctx,
        "chunk": -(-per // 16) * 16,
        "blocks": blocks,
    }
    return jax.shard_map(
        functools.partial(build, cfg),
        mesh=mesh,
        in_specs=(
            P("ctx", "tp"),
            P("tp"),
            P("tp"),
            P(None, "tp"),
            P(None, "tp"),
            P(None, "tp"),
            P("tp", None),
            P(),
            P(),
        ),
        out_specs=P("ctx", "tp"),
        check_vma=False,
    )
```

```python
import functools
import math

import jax
import jax.numpy as jnp
from jax import lax
from jax.experimental import pallas as pl
from jax.experimental.pallas import tpu as pltpu
from jax.sharding import PartitionSpec as P

HD = 64
EPSILON = 1e-05
NEG_FILL = -1e30
MESH = pl.DeviceIdType.MESH
BF16 = jnp.bfloat16
F32 = jnp.float32
I32 = jnp.int32
VMEM_BYTES = 60 * 1024 * 1024


def iota(shape, dim):
    return lax.broadcasted_iota(I32, shape, dim)


def one_hot(mask):
    return jnp.where(mask, 1.0, 0.0).astype(BF16)


def dot(a, b):
    return jnp.dot(a, b, preferred_element_type=F32)


def dot_t(a, b):
    return lax.dot_general(a, b, (((1,), (1,)), ((), ())), preferred_element_type=F32)


def remote(src, dst, send, recv, **where):
    return pltpu.make_async_remote_copy(
        src_ref=src, dst_ref=dst, send_sem=send, recv_sem=recv, device_id=where, device_id_type=MESH
    )


class RingGather:
    def __init__(self, n, pos, core, view, ss, rs, device, sibling, parts=2):
        self.n, self.pos, self.core, self.view, self.ss, self.rs = n, pos, core, view, ss, rs
        self.device, self.sibling, self.parts = device, sibling, parts
        self.sent = []

    def at(self, step):
        return lax.rem(self.pos + step + self.n, self.n)

    def copy(self, pos, which, part, target):
        view = self.view(pos, which, part)
        return remote(view, view, self.ss(len(self.sent)), self.rs(pos, which, part), **target)

    def send(self, pos, part, target):
        copy = self.copy(pos, self.core, part, target)
        copy.start()
        self.sent.append(copy)

    def wait(self, pos, which, part):
        view = self.view(pos, which, part)
        remote(view, view, self.ss(0), self.rs(pos, which, part), **self.sibling).wait_recv()

    def start(self):
        right, left = self.device(self.at(1)), self.device(self.at(-1))
        parts = range(self.parts)
        for part in parts:
            if self.n > 1:
                self.send(self.pos, part, right)
            if self.n > 2:
                self.send(self.pos, self.parts - 1 - part, left)
        for part in parts:
            self.send(self.pos, part, self.sibling)

    def near(self):
        if self.n == 1:
            return
        right, left = self.device(self.at(1)), self.device(self.at(-1))
        for turn in range(self.parts):
            for step in (-1, 1) if self.n > 2 else (-1,):
                part = turn if step == -1 else self.parts - 1 - turn
                self.wait(self.at(step), self.core, part)
                if self.n > 2 and (turn == 0 and self.parts == 2 or self.parts == 1 and step == -1):
                    self.send(self.at(step), part, right if step == -1 else left)
                self.send(self.at(step), part, self.sibling)

    def far(self):
        if self.n > 2:
            for part in range(self.parts):
                self.wait(self.at(2), self.core, part)
                self.send(self.at(2), part, self.sibling)

    def from_sibling(self, pos):
        for part in range(self.parts):
            self.wait(pos, 1 - self.core, part)

    def finish(self):
        for copy in self.sent:
            copy.wait_send()


class Gather:
    def __init__(self, n, pos, core, view, ss, rs, device, sibling):
        self.n, self.pos, self.core, self.view, self.ss, self.rs = n, pos, core, view, ss, rs
        self.device, self.sibling = device, sibling
        self.sent = []

    def at(self, step):
        return lax.rem(self.pos + step, self.n)

    def copy(self, pos, which, slot, target):
        view = self.view(pos, which)
        return remote(view, view, self.ss(slot), self.rs(pos, which), **target)

    def send(self, pos, target):
        copy = self.copy(pos, self.core, len(self.sent), target)
        copy.start()
        self.sent.append(copy)

    def steps(self):
        return sorted(range(1, self.n), key=lambda d: min(d, self.n - d))

    def start(self):
        self.send(self.pos, self.sibling)
        for step in self.steps():
            self.send(self.pos, self.device(self.at(step)))

    def pass_on(self, step):
        self.copy(self.at(step), self.core, 0, self.sibling).wait_recv()
        self.send(self.at(step), self.sibling)

    def from_sibling(self, pos):
        self.copy(pos, 1 - self.core, 0, self.sibling).wait_recv()

    def finish(self):
        for copy in self.sent:
            copy.wait_send()


def kernel(
    cfg,
    counts_ref,
    gain_ref,
    router_ref,
    picked_hbm,
    tokens_hbm,
    wq_hbm,
    wk_hbm,
    wv_hbm,
    wo_hbm,
    out_ref,
    picked_ref,
    tokens_ref,
    wq_ref,
    wk_ref,
    wv_ref,
    wo_ref,
    row_send,
    row_recv,
    gathered,
    normed_ref,
    kv_send,
    kv_ref,
    q_send,
    q_recv,
    q_ref,
    value_ref,
    max_ref,
    acc_ref,
    done_ref,
    gated_ref,
    att_send,
    att_recv,
    pair_send,
    pair_recv,
    own_ref,
    part_send,
    part_recv,
    back_send,
    back_recv,
    w_sem,
    row_ss,
    row_rs,
    gat_ss,
    gat_rs,
    kvz_ss,
    kvz_rs,
    qz_ss,
    qz_rs,
    kvy_ss,
    kvy_rs,
    att_ss,
    att_rs,
    pair_ss,
    pair_rs,
    part_ss,
    part_rs,
    back_ss,
    back_rs,
):
    ny, nz, nx = cfg["ny"], cfg["nz"], cfg["nx"]
    rows, chunk, blocks = cfg["rows"], cfg["chunk"], cfg["blocks"]
    ctx, tp = ny * nz, nx * 2
    seq, feats = tokens_ref.shape
    cap = picked_ref.shape[1]
    slots = ctx * chunk
    shift = chunk.bit_length() - 1
    half = rows // 2
    quarter = half // 2
    width = feats * tp
    heads = feats // HD
    zs = nz // 2

    loads = [
        pltpu.make_async_copy(src, dst, w_sem.at[i])
        for i, (src, dst) in enumerate(
            (
                (picked_hbm, picked_ref),
                (tokens_hbm, tokens_ref),
                (wk_hbm, wk_ref),
                (wv_hbm, wv_ref),
                (wq_hbm, wq_ref),
                (wo_hbm, wo_ref),
            )
        )
    ]
    for copy in loads:
        copy.start()

    c = lax.axis_index("ctx")
    t = lax.axis_index("tp")
    y, z = c // nz, lax.rem(c, nz)
    x, core = t // 2, lax.rem(t, 2)
    sibling = x * 2 + 1 - core

    barrier = pltpu.get_barrier_semaphore()

    def greet(i, _):
        pl.semaphore_signal(
            barrier, inc=1, device_id={"ctx": lax.rem(c + i, ctx)}, device_id_type=MESH
        )
        return 0

    lax.fori_loop(1, ctx, greet, 0)
    for dx in range(1, nx):
        pl.semaphore_signal(
            barrier,
            inc=1,
            device_id={"tp": lax.rem(x + dx, nx) * 2 + core},
            device_id_type=MESH,
        )
    pl.semaphore_signal(barrier, inc=1, device_id={"tp": sibling}, device_id_type=MESH)
    for dz in range(1, nz):
        pl.semaphore_signal(
            barrier,
            inc=1,
            device_id={"ctx": y * nz + lax.rem(z + dz, nz), "tp": sibling},
            device_id_type=MESH,
        )

    own_count = counts_ref[c]
    own_offset = jnp.int32(0)
    for i in range(ctx):
        own_offset = own_offset + jnp.where(i < c, counts_ref[i], 0)
    loads[0].wait()
    place_row = picked_ref[pl.ds(c, 1), :] - c * seq
    place_col = jnp.broadcast_to(place_row, (8, cap)).T[:, :1]
    live_row = iota((1, cap), 1) < own_count
    live_col = iota((cap, 1), 0) < own_count
    before_row = jnp.where(live_col & (place_col < place_row), 1.0, 0.0)
    order_row = jnp.where(live_row, jnp.sum(before_row, axis=0, keepdims=True).astype(I32), -1)

    def wanted(index):
        dest, number = index >> shift, index & (chunk - 1)
        return ((dest - own_offset) & (ctx - 1)) + ctx * number

    deal = one_hot(wanted(iota((slots, 1), 0)) == order_row)
    pick = one_hot(place_col == iota((cap, seq), 1))
    loads[1].wait()
    picked_rows = dot(pick, tokens_ref[...]).astype(BF16)
    row_send[...] = dot(deal, picked_rows).astype(BF16)

    pl.semaphore_wait(barrier, ctx - 1 + nx + nz - 1)

    def span(i):
        return pl.ds(pl.multiple_of(i * chunk, chunk), chunk)

    def exchange(send_ref, recv_ref, ss, rs):
        def begin(i, _):
            d = lax.rem(c + i, ctx)
            remote(
                send_ref.at[span(d)], recv_ref.at[span(c)], ss.at[d], rs.at[c], ctx=d
            ).start()
            return 0

        lax.fori_loop(1, ctx, begin, 0)
        recv_ref[span(c), :] = send_ref[span(c), :]

    def exchange_wait(send_ref, recv_ref, ss, rs):
        def end(i, _):
            d = lax.rem(c + i, ctx)
            remote(send_ref.at[span(d)], recv_ref.at[span(d)], ss.at[d], rs.at[d], ctx=d).wait()
            return 0

        lax.fori_loop(1, ctx, end, 0)

    exchange(row_send, row_recv, row_ss, row_rs)

    source = iota((8, slots), 1) >> shift
    offset_of = jnp.zeros((8, slots), I32)
    count_of = jnp.zeros((8, slots), I32)
    for i in range(ctx):
        count = counts_ref[i]
        offset_of = offset_of + jnp.where(source > i, count, 0)
        count_of = count_of + jnp.where(source == i, count, 0)
    number = ((c - offset_of) & (ctx - 1)) + ctx * (iota((8, slots), 1) & (chunk - 1))
    local_index = jnp.where(number < count_of, (offset_of + number - c) >> (ctx.bit_length() - 1), -1)
    compact = one_hot(local_index[:1] == iota((rows, slots), 0))
    spread_index = local_index.T[:, :1]
    spread = one_hot(spread_index == iota((slots, rows), 1))

    before_col = jnp.where(live_row & (place_row < place_col), 1.0, 0.0)
    order_col = jnp.where(live_col, jnp.sum(before_col, axis=1, keepdims=True).astype(I32), -1)
    undeal = one_hot(order_col == wanted(iota((1, slots), 1)))

    exchange_wait(row_send, row_recv, row_ss, row_rs)

    packed_rows = dot(compact, row_recv[...]).astype(BF16)
    params = jnp.concatenate(
        [
            gain_ref[...].astype(F32).reshape(1, feats),
            router_ref[...].astype(F32).reshape(1, feats),
            jnp.zeros((14, feats), F32),
        ],
        axis=0,
    )
    gathered[0, t, pl.ds(0, half), :] = packed_rows[:half]
    gathered[0, t, pl.ds(half, 16), :] = params.astype(BF16)
    gathered[1, t, pl.ds(0, half), :] = packed_rows[half:]

    def feature_gather(p):
        height = half + 16 if p == 0 else half
        return Gather(
            nx,
            x,
            core,
            lambda pos, which: gathered.at[p, pos * 2 + which, pl.ds(0, height), :],
            lambda slot: gat_ss.at[p, slot],
            lambda pos, which: gat_rs.at[p, pos, which],
            lambda pos: {"tp": pos * 2 + core},
            {"tp": sibling},
        )

    features = [feature_gather(0), feature_gather(1)]
    features[0].start()
    features[1].start()

    zi, parity = z // 2, lax.rem(z, 2)
    head_core = z // heads
    own_head = lax.rem(z, heads)

    def stays(h):
        return (heads * core + h == z) & (parity == core)

    def came(source):
        return (source * 2 + core == z) & (head_core == core)

    def to_head(h, src, dst, ss, rs):
        return remote(src, dst, ss, rs, ctx=y * nz + heads * core + h, tp=x * 2 + parity)

    def to_source(source, src, dst, ss, rs):
        return remote(src, dst, ss, rs, ctx=y * nz + source * 2 + core, tp=x * 2 + head_core)

    def kv_at(p, source, which):
        return kv_ref.at[y, which, p, source]

    def q_at(p, source, which):
        return q_recv.at[p, source]

    def deal_heads(p, send_ref, target, ss, rs):
        for h in range(heads):

            @pl.when(stays(h))
            def _():
                target(p, zi, core)[...] = send_ref[p, h]

            @pl.when(jnp.logical_not(stays(h)))
            def _():
                to_head(h, send_ref.at[p, h], target(p, zi, parity), ss.at[p, h], rs.at[p, zi]).start()

    def deal_heads_wait(p, send_ref, target, ss, rs):
        for source in range(zs):

            @pl.when(jnp.logical_not(came(source)))
            def _():
                to_source(
                    source, send_ref.at[p, 0], target(p, source, core), ss.at[p, 0], rs.at[p, source]
                ).wait_recv()

    def deal_heads_sent(p, send_ref, target, ss, rs):
        for h in range(heads):

            @pl.when(jnp.logical_not(stays(h)))
            def _():
                to_head(h, send_ref.at[p, h], target(p, zi, parity), ss.at[p, h], rs.at[p, zi]).wait_send()

    def project(p):
        squares = jnp.zeros((half, feats), F32)
        routes = jnp.zeros((half, feats), F32)
        for b in range(tp):
            wide = gathered[p, b, pl.ds(0, half), :].astype(F32)
            params = gathered[0, b, pl.ds(half, 16), :].astype(F32)
            squares = squares + wide * wide
            routes = routes + wide * params[1:2]
        scale = lax.rsqrt(jnp.sum(squares, axis=1, keepdims=True) / width + EPSILON)
        for b in range(tp):
            wide = gathered[p, b, pl.ds(0, half), :].astype(F32)
            params = gathered[0, b, pl.ds(half, 16), :].astype(F32)
            normed_ref[p, :, pl.ds(b * feats, feats)] = (wide * scale * params[0:1]).astype(BF16)
        normed = normed_ref[p]
        keys = dot(normed, wk_ref[...]).astype(BF16)
        values = dot(normed, wv_ref[...]).astype(BF16)
        for h in range(heads):
            cols = slice(h * HD, (h + 1) * HD)
            kv_send[p, h] = jnp.concatenate([keys[:, cols], values[:, cols]], axis=1)
        deal_heads(p, kv_send, kv_at, kvz_ss, kvz_rs)
        queries = (dot(normed, wq_ref[...]).astype(BF16).astype(F32) * (1.0 / math.sqrt(HD))).astype(BF16)
        for h in range(heads):
            cols = slice(h * HD, (h + 1) * HD)
            q_send[p, h] = jnp.concatenate([queries[:quarter, cols], queries[quarter:, cols]], axis=1)
        deal_heads(p, q_send, q_at, qz_ss, qz_rs)
        return 1.0 / (1.0 + jnp.exp(-jnp.sum(routes, axis=1, keepdims=True)))

    def gather_end(p):
        for step in features[p].steps():
            features[p].pass_on(step)
        for pos in range(nx):
            features[p].from_sibling(pos)

    gather_end(0)
    for copy in loads[2:]:
        copy.wait()
    gating = [project(0)]
    gather_end(1)
    gating.append(project(1))

    kv_parts = 2 if zs > 1 else 1

    def kv_gather(p):
        split = (zs + 1) // 2
        return RingGather(
            ny,
            y,
            core,
            lambda pos, which, part: kv_ref.at[
                pos, which, p, pl.ds(0, split) if part == 0 else pl.ds(split, zs - split)
            ],
            lambda slot: kvy_ss.at[p, slot],
            lambda pos, which, part: kvy_rs.at[p, pos, which, part],
            lambda pos: {"ctx": pos * nz + z},
            {"tp": sibling},
            parts=kv_parts,
        )

    blocks_kv = [kv_gather(0), kv_gather(1)]
    size = half // blocks
    tile = zs * size
    tile_row = iota((tile, 1), 0)
    tile_col = iota((1, tile), 1)
    query_key = lax.rem(tile_row, size) * ctx + y * nz + (tile_row // size) * 2 + core
    key_base = lax.rem(tile_col, size) * ctx + (tile_col // size) * 2
    value_lane = iota((1, 1, 2 * HD), 2) >= HD
    zeros = jnp.zeros((quarter, HD), BF16)

    def queries_in(p):
        deal_heads_wait(p, q_send, q_at, qz_ss, qz_rs)
        for source in range(zs):
            packed = q_recv[p, source]
            q_ref[p, source, pl.ds(0, quarter), :] = jnp.concatenate([packed[:, :HD], zeros], axis=1)
            q_ref[p, source, pl.ds(quarter, quarter), :] = jnp.concatenate([packed[:, HD:], zeros], axis=1)

    def attend(p, pairs, first=False):
        allowed = []
        for pos, which in pairs:
            value_ref[pos, which, p] = jnp.where(value_lane, kv_ref[pos, which, p], jnp.ones((), BF16))
            allowed.append(key_base + (pos * nz + which) <= query_key)
        for b in range(blocks):
            now = pl.ds(b * size, size)
            q = q_ref[p, :, now, :].reshape(tile, 2 * HD)
            scores, operands = [], []
            for i, (pos, which) in enumerate(pairs):
                near = kv_ref[pos, which, p, :, now, :].reshape(tile, 2 * HD)
                scores.append(jnp.where(allowed[i], dot_t(q, near), NEG_FILL))
                operands.append(value_ref[pos, which, p, :, now, :].reshape(tile, 2 * HD))
                if b:
                    before = pl.ds(0, b * size)
                    past = kv_ref[pos, which, p, :, before, :].reshape(b * tile, 2 * HD)
                    scores.append(dot_t(q, past))
                    operands.append(value_ref[pos, which, p, :, before, :].reshape(b * tile, 2 * HD))
                if p:
                    scores.append(dot_t(q, kv_ref[pos, which, 0].reshape(zs * half, 2 * HD)))
                    operands.append(value_ref[pos, which, 0].reshape(zs * half, 2 * HD))
            peak = None if first else max_ref[p, b]
            for score in scores:
                top = jnp.max(score, axis=1, keepdims=True)
                peak = top if peak is None else jnp.maximum(peak, top)
            product = None if first else acc_ref[p, b] * jnp.exp(max_ref[p, b] - peak)
            for score, operand in zip(scores, operands):
                term = dot(jnp.exp(score - peak).astype(BF16), operand)
                product = term if product is None else product + term
            max_ref[p, b] = peak
            acc_ref[p, b] = product

    def back_start(p):
        for b in range(blocks):
            sums = acc_ref[p, b]
            result = sums[:, HD:] / sums[:, :HD]
            done_ref[p, :, pl.ds(b * size, size), :] = result.astype(BF16).reshape(zs, size, HD)
        for source in range(zs):
            att_send[p, source] = jnp.concatenate(
                [done_ref[p, source, pl.ds(0, quarter), :], done_ref[p, source, pl.ds(quarter, quarter), :]], axis=1
            )
        for source in range(zs):

            @pl.when(came(source))
            def _():
                att_recv[p, own_head] = att_send[p, source]

            @pl.when(jnp.logical_not(came(source)))
            def _():
                back_copy(p, source).start()

    def back_copy(p, source):
        return to_source(
            source, att_send.at[p, source], att_recv.at[p, own_head], att_ss.at[p, source], att_rs.at[p, own_head]
        )

    def back_wait(p):
        for h in range(heads):

            @pl.when(jnp.logical_not(stays(h)))
            def _():
                to_head(h, att_send.at[p, 0], att_recv.at[p, h], att_ss.at[p, 0], att_rs.at[p, h]).wait_recv()

    def columns(index):
        return pl.ds(pl.multiple_of(index * feats, feats), feats)

    pair_order = [2, 1, 3, 0] if nx == 4 else [1, 0] if nx == 2 else [0]
    pair_copies = [[None] * nx, [None] * nx]
    part_copies = [[], []]

    def pair_sums(p):
        joined = [att_recv[p, h] for h in range(heads)]
        attended = jnp.concatenate(
            [
                jnp.concatenate([packed[:, :HD] for packed in joined], axis=1),
                jnp.concatenate([packed[:, HD:] for packed in joined], axis=1),
            ],
            axis=0,
        )
        for dx in pair_order:
            other = lax.rem(x + dx, nx)
            pair_send[p, dx] = dot(attended, wo_ref[:, columns(other * 2 + 1 - core)]).astype(BF16)
            copy = remote(
                pair_send.at[p, dx], pair_recv.at[p, dx], pair_ss.at[p, dx], pair_rs.at[p, dx], tp=sibling
            )
            copy.start()
            pair_copies[p][dx] = copy
        for dx in pair_order:
            other = lax.rem(x + dx, nx)
            own_ref[p, dx] = dot(attended, wo_ref[:, columns(other * 2 + core)])

    def part_sums(p):
        for dx in pair_order[:-1]:
            other = lax.rem(x + dx, nx)
            pair_copies[p][dx].wait()
            part_send[p, dx] = (own_ref[p, dx] + pair_recv[p, dx].astype(F32)).astype(BF16)
            copy = remote(
                part_send.at[p, dx], part_recv.at[p, dx], part_ss.at[p, dx], part_rs.at[p, dx], tp=other * 2 + core
            )
            copy.start()
            part_copies[p].append(copy)

    def finish_rows(p):
        pair_copies[p][0].wait()
        projected = own_ref[p, 0] + pair_recv[p, 0].astype(F32)
        for copy in part_copies[p]:
            copy.wait()
        for dx in range(1, nx):
            projected = projected + part_recv[p, dx].astype(F32)
        gated_ref[pl.ds(p * half, half), :] = (gating[p] * projected).astype(BF16)

    near_by = [lax.rem(y + d, ny) for d in range(1, ny, 2)]
    far_off = [lax.rem(y + d, ny) for d in range(2, ny, 2)]

    def keys_in(p):
        deal_heads_wait(p, kv_send, kv_at, kvz_ss, kvz_rs)
        blocks_kv[p].start()

    def attend_own(p):
        blocks_kv[p].from_sibling(y)
        attend(p, [(y, core), (y, 1 - core)], True)

    def attend_near(p):
        if near_by:
            attend(p, [(pos, core) for pos in near_by])

    def attend_near_other(p):
        if near_by:
            for pos in near_by:
                blocks_kv[p].from_sibling(pos)
            attend(p, [(pos, 1 - core) for pos in near_by])

    def attend_far(p):
        for pos in far_off:
            blocks_kv[p].from_sibling(pos)
            attend(p, [(pos, core), (pos, 1 - core)])

    keys_in(0)
    queries_in(0)
    keys_in(1)
    attend_own(0)
    blocks_kv[0].near()
    queries_in(1)
    attend_near(0)
    attend_own(1)
    blocks_kv[0].far()
    blocks_kv[1].near()
    attend_near_other(0)
    attend_far(0)
    back_start(0)
    attend_near(1)
    blocks_kv[1].far()
    attend_near_other(1)
    attend_far(1)
    back_start(1)
    back_wait(0)
    pair_sums(0)
    part_sums(0)
    back_wait(1)
    pair_sums(1)
    part_sums(1)
    finish_rows(0)
    finish_rows(1)

    back_send[...] = dot(spread, gated_ref[...]).astype(BF16)
    exchange(back_send, back_recv, back_ss, back_rs)
    for p in (0, 1):
        features[p].finish()
        blocks_kv[p].finish()
        deal_heads_sent(p, kv_send, kv_at, kvz_ss, kvz_rs)
        deal_heads_sent(p, q_send, q_at, qz_ss, qz_rs)
        for source in range(zs):

            @pl.when(jnp.logical_not(came(source)))
            def _():
                back_copy(p, source).wait_send()

    exchange_wait(back_send, back_recv, back_ss, back_rs)
    out_ref[...] = dot(undeal, back_recv[...]).astype(BF16)


def build(cfg, tokens, router, gain, w_query, w_key, w_value, w_out, counts, picked):
    ny, nz, nx = cfg["ny"], cfg["nz"], cfg["nx"]
    rows, chunk, blocks = cfg["rows"], cfg["chunk"], cfg["blocks"]
    ctx, tp = ny * nz, nx * 2
    feats = tokens.shape[1]
    cap = picked.shape[1]
    slots = ctx * chunk
    half = rows // 2
    width = feats * tp
    heads = feats // HD
    zs = nz // 2
    tile = zs * (half // blocks)
    vmem = pl.BlockSpec(memory_space=pltpu.VMEM)
    hbm = pl.BlockSpec(memory_space=pltpu.HBM)
    dma = pltpu.SemaphoreType.DMA
    return pl.pallas_call(
        functools.partial(kernel, cfg),
        out_shape=jax.ShapeDtypeStruct((cap, feats), BF16),
        in_specs=[pl.BlockSpec(memory_space=pltpu.SMEM)] + [vmem] * 2 + [hbm] * 6,
        out_specs=vmem,
        scratch_shapes=[
            pltpu.VMEM(picked.shape, I32),
            pltpu.VMEM(tokens.shape, BF16),
            pltpu.VMEM((width, feats), BF16),
            pltpu.VMEM((width, feats), BF16),
            pltpu.VMEM((width, feats), BF16),
            pltpu.VMEM((feats, width), BF16),
            pltpu.VMEM((slots, feats), BF16),
            pltpu.VMEM((slots, feats), BF16),
            pltpu.VMEM((2, tp, half + 16, feats), BF16),
            pltpu.VMEM((2, half, width), BF16),
            pltpu.VMEM((2, heads, half, 2 * HD), BF16),
            pltpu.VMEM((ny, 2, 2, zs, half, 2 * HD), BF16),
            pltpu.VMEM((2, heads, half // 2, 2 * HD), BF16),
            pltpu.VMEM((2, zs, half // 2, 2 * HD), BF16),
            pltpu.VMEM((2, zs, half, 2 * HD), BF16),
            pltpu.VMEM((ny, 2, 2, zs, half, 2 * HD), BF16),
            pltpu.VMEM((2, blocks, tile, 1), F32),
            pltpu.VMEM((2, blocks, tile, 2 * HD), F32),
            pltpu.VMEM((2, zs, half, HD), BF16),
            pltpu.VMEM((rows, feats), BF16),
            pltpu.VMEM((2, zs, half // 2, 2 * HD), BF16),
            pltpu.VMEM((2, heads, half // 2, 2 * HD), BF16),
            pltpu.VMEM((2, nx, half, feats), BF16),
            pltpu.VMEM((2, nx, half, feats), BF16),
            pltpu.VMEM((2, nx, half, feats), F32),
            pltpu.VMEM((2, nx, half, feats), BF16),
            pltpu.VMEM((2, nx, half, feats), BF16),
            pltpu.VMEM((slots, feats), BF16),
            pltpu.VMEM((slots, feats), BF16),
            dma((6,)),
            dma((ctx,)),
            dma((ctx,)),
            dma((2, 2 * nx)),
            dma((2, nx, 2)),
            dma((2, heads)),
            dma((2, zs)),
            dma((2, heads)),
            dma((2, zs)),
            dma((2, 4 * ny + 4)),
            dma((2, ny, 2, 2)),
            dma((2, zs)),
            dma((2, heads)),
            dma((2, nx)),
            dma((2, nx)),
            dma((2, nx)),
            dma((2, nx)),
            dma((ctx,)),
            dma((ctx,)),
        ],
        compiler_params=pltpu.CompilerParams(
            collective_id=0, has_side_effects=True, vmem_limit_bytes=VMEM_BYTES
        ),
    )(counts, gain, router, picked, tokens, w_query, w_key, w_value, w_out)


def solution(mesh, nz=8, selected=6144, cap=384, blocks=1):
    ctx, tp = mesh.shape["ctx"], mesh.shape["tp"]
    per = -(-cap // ctx)
    cfg = {
        "ny": ctx // nz,
        "nz": nz,
        "nx": tp // 2,
        "rows": selected // ctx,
        "chunk": -(-per // 16) * 16,
        "blocks": blocks,
    }
    return jax.shard_map(
        functools.partial(build, cfg),
        mesh=mesh,
        in_specs=(
            P("ctx", "tp"),
            P("tp"),
            P("tp"),
            P(None, "tp"),
            P(None, "tp"),
            P(None, "tp"),
            P("tp", None),
            P(),
            P(),
        ),
        out_specs=P("ctx", "tp"),
        check_vma=False,
    )
```
